32 devices in a mesh: section: 4 (over y, x), shard: 8 (over z, core).
Axes of the slice: x: 2, y: 2, z: 4, core: 2. Of those that a mesh axis runs over, the one named last changes fastest.
Arguments:
- rows: bfloat16 [4, 512, 6144], P('section', 'shard'), may hold values from -6 to 6
- expert_ids: int32 [4, 512, 2], P('section', 'shard'), may hold values from 0 to 7, all different within a row; in each aligned block of 64 rows (0 to 63, 64 to 127, ..., all dimensions but the last counted through in order) at most 18 rows name the same one
- gate_probs: float32 [4, 512, 2], P('section', 'shard'), may hold values from 0.1 to 1
- w_gate: bfloat16 [4, 6144, 8192], P('section', None, 'shard'), may hold values from -0.078125 to 0.078125
- w_up: bfloat16 [4, 6144, 8192], P('section', None, 'shard'), may hold values from -0.078125 to 0.078125
- w_down: bfloat16 [4, 8192, 6144], P('section', 'shard'), may hold values from -0.0625 to 0.0625
Outputs:
- handed: bfloat16 [4, 512, 6144], P('section', 'shard')
The draws below stay inside these ranges and needn't reach their ends.
Inputs may be any that keep to these rules, and one draw needn't show every extreme that they name: `expert_ids`: within each section's block of 64 tokens of one shard index, no expert is named by more than 18 tokens, and each token names 2 different experts.
All inputs are finite; a program needn't handle non-finite values.
Results may differ from the reference program's by a relative error of at most 0.011.
Values may be sent and summed in bfloat16 or wider, within the bound.
No kernel may reach another device: no remote copies, remote signals or barrier semaphores. Data moves between devices by JAX's collectives and lax.ppermute only.
A program may use at most 128 MiB of HBM per device.

```python
import math
import jax
import jax.numpy as jnp
import numpy as np
from jax import lax

D = 6144
EXPERTS = 8
TOP = 2
FFW = 8192
TOK_DEV = 64
CAP = 18
TOK_SECTION = 512
HID_DEV = 1024
N_SECTION = 4
N_SHARD = 8


def level_of(stream_key, shape, split, least, high):
    def one(dim, parts):
        steps = jax.random.uniform(jax.random.fold_in(jax.random.fold_in(stream_key, 6), dim), (parts,), jnp.float32, least / len(split), high / len(split))
        return jnp.repeat(jnp.exp(steps), shape[dim] // parts).reshape((-1,) + (1,) * (len(shape) - dim - 1))

    level = one(*split[0])
    for cut in split[1:]:
        level = level * one(*cut)
    return level


def shared_out(key, own, number, rows, number_of, top, bound, slope):
    sequence = jax.random.permutation(key, number_of)
    crowded, usual = load_shares(number_of, rows * top, bound, slope, True), load_shares(number_of, rows * top, bound, slope, False)
    places = jnp.arange(number_of)

    def named(tallies, offset_by):
        used = int((tallies > 0).sum())
        fixed = max(1, used // 4)
        moved = fixed + (places - fixed + offset_by * (used - fixed)) % max(1, number_of - fixed)
        return jnp.zeros((number_of,), jnp.int32).at[sequence[jnp.where(places < fixed, places, moved)]].set(jnp.asarray(tallies, jnp.int32))

    tallies = jnp.where(number % 4 == 0, named(crowded, number // 4), named(usual, number - number // 4 - 1))
    mixed = jax.random.permutation(jax.random.fold_in(own, 3), number_of)
    donor, receiver = mixed[0:number_of // 2 * 2:2], mixed[1:number_of // 2 * 2:2]
    room = jnp.minimum(tallies[donor] - 1, bound - tallies[receiver]) // 2
    room = jnp.where((donor == sequence[0]) | (receiver == sequence[0]) | (tallies[receiver] == 0), 0, jnp.maximum(room, 0))
    moved = jax.random.randint(jax.random.fold_in(own, 4), (number_of // 2,), 0, 1 << 20) % (room + 1)
    tallies = tallies.at[donor].add(-moved).at[receiver].add(moved)
    members = jnp.searchsorted(jnp.cumsum(tallies), jnp.arange(rows * top), side="right").astype(jnp.int32)
    listing = members.reshape(top, rows).T
    listing = listing[jax.random.permutation(jax.random.fold_in(own, 1), rows)]
    offset_by = jax.random.randint(jax.random.fold_in(own, 2), (rows, 1), 0, top)
    return jnp.take_along_axis(listing, (jnp.arange(top)[None, :] + offset_by) % top, axis=1)


def load_shares(number_of, total, limit, skew, full):
    loads = [(1 << 20) // math.isqrt(standing ** skew) + 1 for standing in range(1, number_of + 1)]
    largest = limit if full else min(limit, max(-(-total // number_of), total * loads[0] // sum(loads)))
    least = 1 if total - largest >= number_of - 1 else 0
    counts, rest = [largest] + [least] * (number_of - 1), total - largest - least * (number_of - 1)
    while rest > 0:
        movable = [i for i in range(1, number_of) if counts[i] < largest] or [i for i in range(1, number_of) if counts[i] < limit]
        pool, left = sum([loads[i] for i in movable]), rest
        for i in movable:
            extra = min(limit - counts[i], max(1, left * loads[i] // pool), rest)
            counts[i] = counts[i] + extra
            rest = rest - extra
    return np.array(counts)


def noise(rng, extent, scale, limit, shards=(), held_as=jnp.bfloat16):
    loudness = level_of(rng, extent, shards, -0.22, 0.18) if shards else 1.0
    result = jax.random.normal(rng, extent, jnp.float32) * scale * loudness
    return jnp.minimum(jnp.maximum(result, -limit), limit).astype(held_as)


def setup_inputs(seed: int = 0) -> dict:
    key_of = jax.random.split(jax.random.key(seed), 7)
    rows = noise(key_of[0], (N_SECTION, TOK_SECTION, D), 1.0, 6.0, ((0, 4), (1, 8)))
    expert_ids_keys = jax.random.split(jax.random.fold_in(key_of[1], 1), N_SECTION * TOK_SECTION // TOK_DEV)
    expert_ids_turns = jax.random.permutation(jax.random.fold_in(key_of[1], 3), N_SECTION * TOK_SECTION // TOK_DEV)
    expert_ids = jax.vmap(lambda own, number: shared_out(jax.random.fold_in(key_of[1], 2), own, number, TOK_DEV, EXPERTS, TOP, CAP, 2))(expert_ids_keys, expert_ids_turns).reshape((N_SECTION, TOK_SECTION, TOP))
    gate_probs = jnp.clip(0.1 + 0.9 * jax.random.uniform(key_of[2], (N_SECTION, TOK_SECTION, TOP), jnp.float32) ** level_of(key_of[2], (N_SECTION, TOK_SECTION, TOP), ((0, 4), (1, 8)), -0.2, 0.2), 0.1, 1.0)
    w_gate = noise(key_of[3], (N_SECTION, D, FFW), D ** -0.5, 0.078125, ((0, 4), (2, 8)))
    w_up = noise(key_of[4], (N_SECTION, D, FFW), D ** -0.5, 0.078125, ((0, 4), (2, 8)))
    w_down = noise(key_of[5], (N_SECTION, FFW, D), FFW ** -0.5, 0.0625, ((0, 4), (1, 8)))
    return dict(rows=rows, expert_ids=expert_ids, gate_probs=gate_probs, w_gate=w_gate, w_up=w_up, w_down=w_down)


def section_layer(tokens, chosen_ids, probs, gate_w, up_w, down_w, section_num):
    hit = chosen_ids == section_num
    routed = jnp.any(hit, axis=-1)
    weight = jnp.sum(jnp.where(hit, probs, jnp.float32(0.0)), axis=-1).astype(jnp.float32)
    blocks = routed.reshape(N_SHARD, TOK_DEV).astype(jnp.int32)
    slot = jnp.cumsum(blocks, axis=1).astype(jnp.int32) - 1
    base = (jnp.arange(N_SHARD, dtype=jnp.int32) * CAP)[:, None]
    dest = jnp.where(blocks > 0, base + slot, N_SHARD * CAP).reshape(-1).astype(jnp.int32)
    packed = jnp.zeros((N_SHARD * CAP + 1, D), jnp.bfloat16).at[dest].set(tokens)[:-1]
    gate = jnp.dot(packed, gate_w, preferred_element_type=jnp.float32)
    upper = jnp.dot(packed, up_w, preferred_element_type=jnp.float32)
    hidden = (jax.nn.silu(gate) * upper).astype(jnp.bfloat16)
    hid_blocks = jnp.transpose(hidden.reshape(N_SHARD * CAP, N_SHARD, HID_DEV), (1, 0, 2))
    down_blocks = down_w.reshape(N_SHARD, HID_DEV, D)

    def add_block(total, pair):
        part = jnp.dot(pair[0], pair[1], preferred_element_type=jnp.float32).astype(jnp.bfloat16)
        part = lax.optimization_barrier(part)
        return total + part.astype(jnp.float32), None

    total, unused = lax.scan(add_block, jnp.zeros((N_SHARD * CAP, D), jnp.float32), (hid_blocks, down_blocks))
    expert_out = total.astype(jnp.bfloat16)
    extended = jnp.concatenate([expert_out, jnp.zeros((1, D), jnp.bfloat16)], axis=0)
    per_token = extended[dest]
    mixed = tokens.astype(jnp.float32) + weight[:, None] * per_token.astype(jnp.float32)
    return mixed.astype(jnp.bfloat16)


def reference(rows, expert_ids, gate_probs, w_gate, w_up, w_down):
    outputs = []
    for section_num in range(N_SECTION):
        outputs.append(section_layer(rows[section_num], expert_ids[section_num], gate_probs[section_num], w_gate[section_num], w_up[section_num], w_down[section_num], section_num))
    stacked = jnp.stack(outputs, axis=0)
    return jnp.roll(stacked, 1, axis=0)
```

```python
import jax
import jax.numpy as jnp
from jax import lax
from jax.experimental import pallas as pl
from jax.experimental.pallas import tpu as pltpu
from jax.sharding import PartitionSpec as P

CAP = 18
MAIN = 16
SLABS = 8
CHUNKS = 2
VMEM_LIMIT = 12 * 1024 * 1024


def params():
    return pltpu.CompilerParams(vmem_limit_bytes=VMEM_LIMIT)


def cost(flops, moved):
    return pl.CostEstimate(flops=flops, bytes_accessed=moved, transcendentals=0)


def whole(count):
    return [pl.BlockSpec(memory_space=pltpu.VMEM)] * count


def pack_kernel(section_ref, ids_ref, probs_ref, tokens_ref, info_ref, *packed_refs):
    section = section_ref[0]
    hit = (ids_ref[...] == section).astype(jnp.float32)
    tokens_count = hit.shape[1]
    routed = jnp.max(hit, axis=0, keepdims=True)
    weight = jnp.sum(hit * probs_ref[...], axis=0, keepdims=True)
    row = lax.broadcasted_iota(jnp.int32, (tokens_count, tokens_count), 0)
    col = lax.broadcasted_iota(jnp.int32, (tokens_count, tokens_count), 1)
    before = (row <= col).astype(jnp.bfloat16)
    counted = jnp.dot(
        jnp.broadcast_to(routed, (MAIN, tokens_count)).astype(jnp.bfloat16),
        before,
        preferred_element_type=jnp.float32,
    )[:1]
    slot = jnp.where(routed > 0.0, counted - 1.0, -1.0)
    out_row = lax.broadcasted_iota(jnp.int32, (2 * MAIN, tokens_count), 0)
    wanted = jnp.where(out_row < MAIN, out_row, MAIN + (out_row - MAIN) // SLABS)
    placed = slot == wanted.astype(jnp.float32)
    width = tokens_ref.shape[1] // CHUNKS
    slab = width // SLABS
    for c in range(CHUNKS):
        rest = jnp.zeros((MAIN, slab), jnp.float32)
        for k in range(SLABS):
            keep = placed & ((out_row < MAIN) | (out_row % SLABS == k))
            mark = jnp.where(keep, 1.0, 0.0).astype(jnp.bfloat16)
            start = c * width + k * slab
            got = jnp.dot(mark, tokens_ref[:, start : start + slab], preferred_element_type=jnp.float32)
            packed_refs[c][:, k * slab : (k + 1) * slab] = got[:MAIN].astype(jnp.bfloat16)
            rest = rest + got[MAIN:]
        packed_refs[c][:, width:] = rest.astype(jnp.bfloat16)
    high = weight.astype(jnp.bfloat16).astype(jnp.float32)
    middle = (weight - high).astype(jnp.bfloat16).astype(jnp.float32)
    low = weight - high - middle
    kind = lax.broadcasted_iota(jnp.int32, (128, tokens_count), 0) % 8
    values = jnp.where(kind == 0, slot, jnp.where(kind == 1, high, jnp.where(kind == 2, middle, low)))
    values = jnp.where(kind < 4, values, 0.0).T
    token = lax.broadcasted_iota(jnp.int32, (tokens_count, 128), 0)
    lane = lax.broadcasted_iota(jnp.int32, (tokens_count, 128), 1)
    values = jnp.where(lane // 8 == token // MAIN, values, 0.0).astype(jnp.bfloat16)
    fold_row = lax.broadcasted_iota(jnp.int32, (MAIN, tokens_count), 0)
    fold_col = lax.broadcasted_iota(jnp.int32, (MAIN, tokens_count), 1)
    fold = (fold_col % MAIN == fold_row).astype(jnp.bfloat16)
    info_ref[...] = jnp.dot(fold, values, preferred_element_type=jnp.float32).astype(jnp.bfloat16)


def fetch_kernel(after_ref, *refs):
    count = len(refs) // 2
    sources, targets, sems = refs[:count], refs[count : 2 * count], refs[-1]
    copies = []
    for a in range(count):
        rows = sources[a].shape[0]
        step = rows // 8
        for i in range(8):
            part = pl.ds(i * step, step)
            copies.append(
                pltpu.make_async_copy(sources[a].at[part], targets[a].at[part], sems.at[a, i])
            )
    for copy in copies:
        copy.start()
    for copy in copies:
        copy.wait()


def regroup(blocks, back):
    size = blocks * 2 * SLABS
    r = lax.broadcasted_iota(jnp.int32, (size, size), 1 if back else 0)
    q = lax.broadcasted_iota(jnp.int32, (size, size), 0 if back else 1)
    slab, pair = r // (2 * blocks), r % (2 * blocks)
    return (q == pair * SLABS + slab).astype(jnp.bfloat16)


def gather_rows(block_refs, x_ref):
    blocks = len(block_refs)
    width = x_ref.shape[1]
    slab = width // SLABS
    for b, ref in enumerate(block_refs):
        x_ref[b * MAIN : (b + 1) * MAIN, :] = ref[:, :width]
    rest = jnp.concatenate([ref[:, width:] for ref in block_refs], axis=0)
    rest = jnp.dot(regroup(blocks, False), rest, preferred_element_type=jnp.float32).astype(jnp.bfloat16)
    for k in range(SLABS):
        x_ref[blocks * MAIN :, k * slab : (k + 1) * slab] = rest[k * 2 * blocks : (k + 1) * 2 * blocks]


def first_kernel(blocks, chunk, *refs):
    block_refs = refs[:blocks]
    w_gate_ref, w_up_ref, gate_ref, up_ref, x_ref = refs[blocks:]
    gather_rows(block_refs, x_ref)
    depth = x_ref.shape[1]
    part = slice(chunk * depth, (chunk + 1) * depth)
    gate_ref[...] = jnp.dot(x_ref[...], w_gate_ref[part, :], preferred_element_type=jnp.float32)
    up_ref[...] = jnp.dot(x_ref[...], w_up_ref[part, :], preferred_element_type=jnp.float32)


def last_kernel(blocks, chunk, *refs):
    block_refs = refs[:blocks]
    w_gate_ref, w_up_ref, gate_ref, up_ref, hidden_ref, x_ref = refs[blocks:]
    gather_rows(block_refs, x_ref)
    depth = x_ref.shape[1]
    part = slice(chunk * depth, (chunk + 1) * depth)
    gate = gate_ref[...] + jnp.dot(x_ref[...], w_gate_ref[part, :], preferred_element_type=jnp.float32)
    upper = up_ref[...] + jnp.dot(x_ref[...], w_up_ref[part, :], preferred_element_type=jnp.float32)
    hidden_ref[...] = (gate / (1.0 + jnp.exp(-gate)) * upper).astype(jnp.bfloat16)


def down_kernel(blocks, chunk, hidden_ref, w_down_ref, own_ref, other_ref):
    half = blocks // 2 * MAIN
    width = w_down_ref.shape[1] // CHUNKS
    slab = width // SLABS
    part = slice(chunk * width, (chunk + 1) * width)
    got = jnp.dot(hidden_ref[...], w_down_ref[:, part], preferred_element_type=jnp.float32)
    main = blocks * MAIN
    own_ref[:, :width] = got[:half].astype(own_ref.dtype)
    other_ref[:, :width] = got[half:main].astype(jnp.bfloat16)
    rest = got[main:].astype(jnp.bfloat16)
    stacked = jnp.concatenate([rest[:, k * slab : (k + 1) * slab] for k in range(SLABS)], axis=0)
    rest = jnp.dot(regroup(blocks, True), stacked, preferred_element_type=jnp.float32)
    own_ref[:, width:] = rest[:half].astype(own_ref.dtype)
    other_ref[:, width:] = rest[half:].astype(jnp.bfloat16)


def add_kernel(own_ref, other_ref, *out_refs):
    total = own_ref[...].astype(jnp.float32) + other_ref[...].astype(jnp.float32)
    for m, ref in enumerate(out_refs):
        ref[...] = total[m * MAIN : (m + 1) * MAIN].astype(ref.dtype)


def sum_kernel(parts, *refs):
    out_ref = refs[-1]
    total = refs[0][...]
    for ref in refs[1:parts]:
        total = total + ref[...].astype(jnp.float32)
    width = total.shape[1]
    out_ref[:, :width] = total.astype(jnp.bfloat16)
    if len(refs) > parts + 1:
        out_ref[:, width:] = refs[parts][...]


def final_kernel(rows_ref, *refs):
    out_ref = refs[-1]
    count = rows_ref.shape[0]
    width = rows_ref.shape[1] // CHUNKS
    slab = width // SLABS
    wide = width + slab
    token = lax.broadcasted_iota(jnp.int32, (count, MAIN), 0)
    column = lax.broadcasted_iota(jnp.int32, (count, MAIN), 1)
    unfold = (token % MAIN == column).astype(jnp.bfloat16)
    info = jnp.dot(unfold, refs[0][:, wide:], preferred_element_type=jnp.float32)
    token = lax.broadcasted_iota(jnp.int32, info.shape, 0)
    lane = lax.broadcasted_iota(jnp.int32, info.shape, 1)
    info = jnp.where(lane // 8 == token // MAIN, info, 0.0)
    slot = jnp.sum(jnp.where(lane % 8 == 0, info, 0.0), axis=1, keepdims=True)
    weight = jnp.sum(jnp.where(lane % 8 == 0, 0.0, info), axis=1, keepdims=True)
    wanted = jnp.where(lane < MAIN, lane, MAIN + (lane - MAIN) // SLABS)
    placed = (slot == wanted.astype(jnp.float32)) & (lane < 2 * MAIN)
    for k in range(SLABS):
        keep = placed & ((lane < MAIN) | (lane % SLABS == k))
        mark = jnp.where(keep, 1.0, 0.0).astype(jnp.bfloat16)[:, : 2 * MAIN]
        for c in range(CHUNKS):
            ref = refs[c]
            values = jnp.concatenate([ref[:, k * slab : (k + 1) * slab], ref[:, width:wide]], axis=0)
            moved = jnp.dot(mark, values, preferred_element_type=jnp.float32)
            span = slice(c * width + k * slab, c * width + (k + 1) * slab)
            out_ref[:, span] = (rows_ref[:, span].astype(jnp.float32) + weight * moved).astype(jnp.bfloat16)


def on_device(rows, expert_ids, gate_probs, w_gate, w_up, w_down):
    bf16, f32 = jnp.bfloat16, jnp.float32
    tokens = rows[0]
    count, model = tokens.shape
    hidden_units = w_gate.shape[2]
    shards = lax.axis_size("shard")
    sections = lax.axis_size("section")
    chips = shards // 2
    width = model // CHUNKS
    wide = width + width // SLABS
    total_rows = shards * CAP

    def along(value, steps):
        return lax.ppermute(value, "shard", [(i, (i + 2 * steps) % shards) for i in range(shards)])

    def swap(value):
        return lax.ppermute(value, "shard", [(i, i ^ 1) for i in range(shards)])

    def onward(value):
        return lax.ppermute(value, "section", [(s, (s + 1) % sections) for s in range(sections)])

    section = lax.axis_index("section").astype(jnp.int32).reshape(1)
    info, *packed = pl.pallas_call(
        pack_kernel,
        out_shape=[jax.ShapeDtypeStruct((MAIN, 128), bf16)]
        + [jax.ShapeDtypeStruct((MAIN, wide), bf16)] * CHUNKS,
        in_specs=[pl.BlockSpec(memory_space=pltpu.SMEM)] + whole(3),
        out_specs=whole(1 + CHUNKS),
        compiler_params=params(),
        cost_estimate=cost(0, 4 * count * model),
        name="pack",
    )(section, expert_ids[0].T, gate_probs[0].T, tokens)

    mine = [[packed[c]] + [along(packed[c], m) for m in range(1, chips)] for c in range(CHUNKS)]
    rows_in = onward(tokens)

    gate_w, up_w, down_w = pl.pallas_call(
        fetch_kernel,
        out_shape=[
            pltpu.VMEM((model, hidden_units), bf16),
            pltpu.VMEM((model, hidden_units), bf16),
            pltpu.VMEM((hidden_units, model), bf16),
        ],
        in_specs=[pl.BlockSpec(memory_space=pl.ANY)] * 4,
        out_specs=whole(3),
        scratch_shapes=[pltpu.SemaphoreType.DMA((3, 8))],
        compiler_params=params(),
        cost_estimate=cost(0, 2 * 3 * 2 * model * hidden_units),
        name="fetch",
    )(packed[0], w_gate[0], w_up[0], w_down[0])

    acc = jax.ShapeDtypeStruct((total_rows, hidden_units), f32)
    state = []
    for c in range(CHUNKS):
        blocks = mine[c] + [swap(block) for block in mine[c]]
        last = c == CHUNKS - 1
        body = last_kernel if last else first_kernel
        state = pl.pallas_call(
            lambda *refs, body=body, c=c: body(shards, c, *refs),
            out_shape=[jax.ShapeDtypeStruct((total_rows, hidden_units), bf16)] if last else [acc, acc],
            in_specs=whole(shards + 2 + len(state)),
            out_specs=whole(1 if last else 2),
            scratch_shapes=[pltpu.VMEM((total_rows, width), bf16)],
            compiler_params=params(),
            cost_estimate=cost(4 * total_rows * width * hidden_units, 4 * width * hidden_units),
            name="hidden" if last else "gate_up",
        )(*blocks, gate_w, up_w, *state)
    hidden = state[0]

    halves = []
    for c in range(CHUNKS):
        own, other = pl.pallas_call(
            lambda *refs, c=c: down_kernel(shards, c, *refs),
            out_shape=[
                jax.ShapeDtypeStruct((chips * MAIN, wide), f32),
                jax.ShapeDtypeStruct((chips * MAIN, wide), bf16),
            ],
            in_specs=whole(2),
            out_specs=whole(2),
            compiler_params=params(),
            cost_estimate=cost(2 * total_rows * width * hidden_units, 2 * width * hidden_units),
            name="down",
        )(hidden, down_w)
        halves.append((own, swap(other)))
    arrived = []
    for c, (own, other) in enumerate(halves):
        kept, *leaving = pl.pallas_call(
            add_kernel,
            out_shape=[jax.ShapeDtypeStruct((MAIN, wide), f32)]
            + [jax.ShapeDtypeStruct((MAIN, wide), bf16)] * (chips - 1),
            in_specs=whole(2),
            out_specs=whole(chips),
            compiler_params=params(),
            name="add_cores",
        )(own, other)
        coming = [along(block, -m) for m, block in enumerate(leaving, 1)]
        extra = [info] if c == 0 else []
        summed = pl.pallas_call(
            lambda *refs: sum_kernel(chips, *refs),
            out_shape=jax.ShapeDtypeStruct((MAIN, wide + 128 * len(extra)), bf16),
            in_specs=whole(chips + len(extra)),
            out_specs=pl.BlockSpec(memory_space=pltpu.VMEM),
            compiler_params=params(),
            name="sum_chips",
        )(kept, *coming, *extra)
        arrived.append(onward(summed))
    out = pl.pallas_call(
        final_kernel,
        out_shape=jax.ShapeDtypeStruct((count, model), bf16),
        in_specs=whole(1 + CHUNKS),
        out_specs=pl.BlockSpec(memory_space=pltpu.VMEM),
        compiler_params=params(),
        name="combine",
    )(rows_in, *arrived)
    return out[None]


def solution(mesh):
    in_specs = (
        P("section", "shard", None),
        P("section", "shard", None),
        P("section", "shard", None),
        P("section", None, "shard"),
        P("section", None, "shard"),
        P("section", "shard", None),
    )
    return jax.shard_map(
        on_device, mesh=mesh, in_specs=in_specs, out_specs=P("section", "shard", None), check_vma=False
    )
```

```python
import jax
import jax.numpy as jnp
from jax import lax
from jax.experimental import pallas as pl
from jax.experimental.pallas import tpu as pltpu
from jax.sharding import PartitionSpec as P

CAP = 18
MAIN = 16
SLABS = 8
CHUNKS = 2
VMEM_LIMIT = 8 * 1024 * 1024


def params():
    return pltpu.CompilerParams(vmem_limit_bytes=VMEM_LIMIT)


def cost(flops, moved):
    return pl.CostEstimate(flops=flops, bytes_accessed=moved, transcendentals=0)


def in_hbm(value):
    return pltpu.with_memory_space_constraint(value, pltpu.HBM)


def in_vmem(value):
    return pltpu.with_memory_space_constraint(value, pltpu.VMEM)


def whole(count):
    return [pl.BlockSpec(memory_space=pltpu.VMEM)] * count


def pack_kernel(section_ref, ids_in, probs_in, tokens_in, info_ref, packed_ref, ids_ref, probs_ref, tokens_ref, sems):
    pairs = ((ids_in, ids_ref), (probs_in, probs_ref), (tokens_in, tokens_ref))
    copies = [pltpu.make_async_copy(a, b, sems.at[i]) for i, (a, b) in enumerate(pairs)]
    for copy in copies:
        copy.start()
    copies[0].wait()
    copies[1].wait()
    section = section_ref[0]
    hit = (ids_ref[...] == section).astype(jnp.float32)
    tokens_count = hit.shape[1]
    routed = jnp.max(hit, axis=0, keepdims=True)
    weight = jnp.sum(hit * probs_ref[...], axis=0, keepdims=True)
    row = lax.broadcasted_iota(jnp.int32, (tokens_count, tokens_count), 0)
    col = lax.broadcasted_iota(jnp.int32, (tokens_count, tokens_count), 1)
    before = (row <= col).astype(jnp.bfloat16)
    counted = jnp.dot(
        jnp.broadcast_to(routed, (MAIN, tokens_count)).astype(jnp.bfloat16),
        before,
        preferred_element_type=jnp.float32,
    )[:1]
    slot = jnp.where(routed > 0.0, counted - 1.0, -1.0)
    out_row = lax.broadcasted_iota(jnp.int32, (2 * MAIN, tokens_count), 0)
    wanted = jnp.where(out_row < MAIN, out_row, MAIN + (out_row - MAIN) // SLABS)
    placed = slot == wanted.astype(jnp.float32)
    width = tokens_ref.shape[1]
    slab = width // SLABS
    copies[2].wait()
    rest = jnp.zeros((MAIN, slab), jnp.float32)
    for k in range(SLABS):
        keep = placed & ((out_row < MAIN) | (out_row % SLABS == k))
        mark = jnp.where(keep, 1.0, 0.0).astype(jnp.bfloat16)
        part = slice(k * slab, (k + 1) * slab)
        got = jnp.dot(mark, tokens_ref[:, part], preferred_element_type=jnp.float32)
        packed_ref[:, part] = got[:MAIN].astype(jnp.bfloat16)
        rest = rest + got[MAIN:]
    packed_ref[:, width:] = rest.astype(jnp.bfloat16)
    high = weight.astype(jnp.bfloat16).astype(jnp.float32)
    middle = (weight - high).astype(jnp.bfloat16).astype(jnp.float32)
    low = weight - high - middle
    kind = lax.broadcasted_iota(jnp.int32, (128, tokens_count), 0) % 8
    values = jnp.where(kind == 0, slot, jnp.where(kind == 1, high, jnp.where(kind == 2, middle, low)))
    values = jnp.where(kind < 4, values, 0.0).T
    token = lax.broadcasted_iota(jnp.int32, (tokens_count, 128), 0)
    lane = lax.broadcasted_iota(jnp.int32, (tokens_count, 128), 1)
    values = jnp.where(lane // 8 == token // MAIN, values, 0.0).astype(jnp.bfloat16)
    fold_row = lax.broadcasted_iota(jnp.int32, (MAIN, tokens_count), 0)
    fold_col = lax.broadcasted_iota(jnp.int32, (MAIN, tokens_count), 1)
    fold = (fold_col % MAIN == fold_row).astype(jnp.bfloat16)
    info_ref[...] = jnp.dot(fold, values, preferred_element_type=jnp.float32).astype(jnp.bfloat16)


def fetch_kernel(after_ref, *refs):
    done_ref, sems = refs[-2:]
    done_ref[...] = jnp.zeros(done_ref.shape, done_ref.dtype)
    copies = []
    for a, (source, target) in enumerate(zip(refs[:3], refs[3:])):
        step = source.shape[0] // 8
        for i in range(8):
            part = pl.ds(i * step, step)
            copies.append(pltpu.make_async_copy(source.at[part], target.at[part], sems.at[a, i]))
    for copy in copies:
        copy.start()
    for copy in copies:
        copy.wait()


def regroup(blocks, back):
    size = blocks * 2 * SLABS
    r = lax.broadcasted_iota(jnp.int32, (size, size), 1 if back else 0)
    q = lax.broadcasted_iota(jnp.int32, (size, size), 0 if back else 1)
    slab, pair = r // (2 * blocks), r % (2 * blocks)
    return (q == pair * SLABS + slab).astype(jnp.bfloat16)


def gather_rows(blocks, mine_ref, other_ref, x_ref):
    width = x_ref.shape[1]
    slab = width // SLABS
    half = blocks // 2 * MAIN
    x_ref[:half, :] = mine_ref[:, :width]
    x_ref[half : 2 * half, :] = other_ref[:, :width]
    rest = jnp.concatenate([mine_ref[:, width:], other_ref[:, width:]], axis=0)
    rest = jnp.dot(regroup(blocks, False), rest, preferred_element_type=jnp.float32).astype(jnp.bfloat16)
    for k in range(SLABS):
        x_ref[blocks * MAIN :, k * slab : (k + 1) * slab] = rest[k * 2 * blocks : (k + 1) * 2 * blocks]


def stack_kernel(blocks, *refs):
    out_ref = refs[-1]
    for b, ref in enumerate(refs[:blocks]):
        out_ref[b * MAIN : (b + 1) * MAIN, :] = ref[...]


def hidden_kernel(blocks, mine_ref, other_ref, w_gate_ref, w_up_ref, hidden_ref, x_ref):
    gather_rows(blocks, mine_ref, other_ref, x_ref)
    gate = jnp.dot(x_ref[...], w_gate_ref[...], preferred_element_type=jnp.float32)
    upper = jnp.dot(x_ref[...], w_up_ref[...], preferred_element_type=jnp.float32)
    hidden_ref[...] = (gate / (1.0 + jnp.exp(-gate)) * upper).astype(jnp.bfloat16)


def down_kernel(blocks, chunk, hidden_ref, w_down_ref, own_ref, other_ref):
    half = blocks // 2 * MAIN
    width = w_down_ref.shape[1] // CHUNKS
    slab = width // SLABS
    part = slice(chunk * width, (chunk + 1) * width)
    got = jnp.dot(hidden_ref[...], w_down_ref[:, part], preferred_element_type=jnp.float32)
    main = blocks * MAIN
    own_ref[:, :width] = got[:half].astype(own_ref.dtype)
    other_ref[:, :width] = got[half:main].astype(jnp.bfloat16)
    rest = got[main:].astype(jnp.bfloat16)
    stacked = jnp.concatenate([rest[:, k * slab : (k + 1) * slab] for k in range(SLABS)], axis=0)
    rest = jnp.dot(regroup(blocks, True), stacked, preferred_element_type=jnp.float32)
    own_ref[:, width:] = rest[:half].astype(own_ref.dtype)
    other_ref[:, width:] = rest[half:].astype(jnp.bfloat16)


def add_kernel(own_ref, other_ref, *out_refs):
    total = own_ref[...].astype(jnp.float32) + other_ref[...].astype(jnp.float32)
    for m, ref in enumerate(out_refs):
        ref[...] = total[m * MAIN : (m + 1) * MAIN].astype(ref.dtype)


def sum_kernel(parts, *refs):
    out_ref = refs[-1]
    total = refs[0][...]
    for ref in refs[1:parts]:
        total = total + ref[...].astype(jnp.float32)
    width = total.shape[1]
    out_ref[:, :width] = total.astype(jnp.bfloat16)
    if len(refs) > parts + 1:
        out_ref[:, width:] = refs[parts][...]


def final_kernel(rows_ref, *refs):
    out_ref = refs[-1]
    count = rows_ref.shape[0]
    width = rows_ref.shape[1] // CHUNKS
    slab = width // SLABS
    wide = width + slab
    token = lax.broadcasted_iota(jnp.int32, (count, MAIN), 0)
    column = lax.broadcasted_iota(jnp.int32, (count, MAIN), 1)
    unfold = (token % MAIN == column).astype(jnp.bfloat16)
    info = jnp.dot(unfold, refs[0][:, wide:], preferred_element_type=jnp.float32)
    token = lax.broadcasted_iota(jnp.int32, info.shape, 0)
    lane = lax.broadcasted_iota(jnp.int32, info.shape, 1)
    info = jnp.where(lane // 8 == token // MAIN, info, 0.0)
    slot = jnp.sum(jnp.where(lane % 8 == 0, info, 0.0), axis=1, keepdims=True)
    weight = jnp.sum(jnp.where(lane % 8 == 0, 0.0, info), axis=1, keepdims=True)
    wanted = jnp.where(lane < MAIN, lane, MAIN + (lane - MAIN) // SLABS)
    placed = (slot == wanted.astype(jnp.float32)) & (lane < 2 * MAIN)
    for k in range(SLABS):
        keep = placed & ((lane < MAIN) | (lane % SLABS == k))
        mark = jnp.where(keep, 1.0, 0.0).astype(jnp.bfloat16)[:, : 2 * MAIN]
        for c in range(CHUNKS):
            ref = refs[c]
            values = jnp.concatenate([ref[:, k * slab : (k + 1) * slab], ref[:, width:wide]], axis=0)
            moved = jnp.dot(mark, values, preferred_element_type=jnp.float32)
            span = slice(c * width + k * slab, c * width + (k + 1) * slab)
            out_ref[:, span] = (rows_ref[:, span].astype(jnp.float32) + weight * moved).astype(jnp.bfloat16)


def on_device(rows, expert_ids, gate_probs, w_gate, w_up, w_down):
    bf16, f32 = jnp.bfloat16, jnp.float32
    _, count, model = rows.shape
    hidden_units = w_gate.shape[2]
    shards = lax.axis_size("shard")
    sections = lax.axis_size("section")
    chips = shards // 2
    width = model // CHUNKS
    wide = width + width // SLABS
    total_rows = shards * CAP

    def along(value, steps):
        return lax.ppermute(value, "shard", [(i, (i + 2 * steps) % shards) for i in range(shards)])

    def swap(value):
        return lax.ppermute(value, "shard", [(i, i ^ 1) for i in range(shards)])

    def onward(value):
        return lax.ppermute(value, "section", [(s, (s + 1) % sections) for s in range(sections)])

    section = lax.axis_index("section").astype(jnp.int32).reshape(1)
    info, packed = pl.pallas_call(
        pack_kernel,
        out_shape=[
            jax.ShapeDtypeStruct((MAIN, 128), bf16),
            jax.ShapeDtypeStruct((MAIN, model + model // SLABS), bf16),
        ],
        in_specs=[pl.BlockSpec(memory_space=pltpu.SMEM)] + [pl.BlockSpec(memory_space=pltpu.HBM)] * 3,
        out_specs=whole(2),
        scratch_shapes=[
            pltpu.VMEM(expert_ids.shape[:0:-1], jnp.int32),
            pltpu.VMEM(gate_probs.shape[:0:-1], f32),
            pltpu.VMEM((count, model), bf16),
            pltpu.SemaphoreType.DMA((3,)),
        ],
        compiler_params=params(),
        cost_estimate=cost(0, 4 * count * model),
        name="pack",
    )(section, in_hbm(expert_ids[0].T), in_hbm(gate_probs[0].T), in_hbm(rows[0]))

    mine = [packed] + [along(packed, m) for m in range(1, chips)]

    gate_w, up_w, down_w, done = pl.pallas_call(
        fetch_kernel,
        out_shape=[
            pltpu.VMEM((model, hidden_units), bf16),
            pltpu.VMEM((model, hidden_units), bf16),
            pltpu.VMEM((hidden_units, model), bf16),
            jax.ShapeDtypeStruct((8, 128), f32),
        ],
        in_specs=[pl.BlockSpec(memory_space=pl.ANY)] + [pl.BlockSpec(memory_space=pltpu.HBM)] * 3,
        out_specs=whole(4),
        scratch_shapes=[pltpu.SemaphoreType.DMA((3, 8))],
        compiler_params=pltpu.CompilerParams(vmem_limit_bytes=12*1024*1024),
        cost_estimate=cost(0, 3 * 2 * 2 * model * hidden_units),
        name="fetch",
    )(packed, in_hbm(w_gate[0]), in_hbm(w_up[0]), in_hbm(w_down[0]))
    rows_in = onward(rows[0])

    held = pl.pallas_call(
        lambda *refs: stack_kernel(chips, *refs),
        out_shape=jax.ShapeDtypeStruct((chips * MAIN, model + model // SLABS), bf16),
        in_specs=whole(chips + 1),
        out_specs=pl.BlockSpec(memory_space=pltpu.VMEM),
        compiler_params=params(),
        name="stack",
    )(*mine, done)
    hidden = pl.pallas_call(
        lambda *refs: hidden_kernel(shards, *refs),
        out_shape=jax.ShapeDtypeStruct((total_rows, hidden_units), bf16),
        in_specs=whole(4),
        out_specs=pl.BlockSpec(memory_space=pltpu.VMEM),
        scratch_shapes=[pltpu.VMEM((total_rows, model), bf16)],
        compiler_params=params(),
        cost_estimate=cost(4 * total_rows * model * hidden_units, 4 * model * hidden_units),
        name="hidden",
    )(held, swap(held), gate_w, up_w)

    halves = []
    for c in range(CHUNKS):
        own, other = pl.pallas_call(
            lambda *refs, c=c: down_kernel(shards, c, *refs),
            out_shape=[
                jax.ShapeDtypeStruct((chips * MAIN, wide), f32),
                jax.ShapeDtypeStruct((chips * MAIN, wide), bf16),
            ],
            in_specs=whole(2),
            out_specs=whole(2),
            compiler_params=params(),
            cost_estimate=cost(2 * total_rows * width * hidden_units, 2 * width * hidden_units),
            name="down",
        )(hidden, down_w)
        halves.append((own, swap(other)))
    arrived = []
    for c, (own, other) in enumerate(halves):
        kept, *leaving = pl.pallas_call(
            add_kernel,
            out_shape=[jax.ShapeDtypeStruct((MAIN, wide), f32)]
            + [jax.ShapeDtypeStruct((MAIN, wide), bf16)] * (chips - 1),
            in_specs=whole(2),
            out_specs=whole(chips),
            compiler_params=params(),
            name="add_cores",
        )(own, other)
        coming = [along(block, -m) for m, block in enumerate(leaving, 1)]
        extra = [info] if c == 0 else []
        summed = pl.pallas_call(
            lambda *refs: sum_kernel(chips, *refs),
            out_shape=jax.ShapeDtypeStruct((MAIN, wide + 128 * len(extra)), bf16),
            in_specs=whole(chips + len(extra)),
            out_specs=pl.BlockSpec(memory_space=pltpu.VMEM),
            compiler_params=params(),
            name="sum_chips",
        )(kept, *coming, *extra)
        arrived.append(onward(summed))
    out = pl.pallas_call(
        final_kernel,
        out_shape=jax.ShapeDtypeStruct((count, model), bf16),
        in_specs=whole(1 + CHUNKS),
        out_specs=pl.BlockSpec(memory_space=pltpu.VMEM),
        compiler_params=params(),
        name="combine",
    )(rows_in, *arrived)
    return out[None]


def solution(mesh):
    in_specs = (
        P("section", "shard", None),
        P("section", "shard", None),
        P("section", "shard", None),
        P("section", None, "shard"),
        P("section", None, "shard"),
        P("section", "shard", None),
    )
    return jax.shard_map(
        on_device, mesh=mesh, in_specs=in_specs, out_specs=P("section", "shard", None), check_vma=False
    )
```

```python
import jax
import jax.numpy as jnp
from jax import lax
from jax.experimental import pallas as pl
from jax.experimental.pallas import tpu as pltpu
from jax.sharding import PartitionSpec as P

CAP = 18
MAIN = 16
SLABS = 8
CHUNKS = (3, 3)
VMEM_LIMIT = 8 * 1024 * 1024


def params():
    return pltpu.CompilerParams(vmem_limit_bytes=VMEM_LIMIT)


def cost(flops, moved):
    return pl.CostEstimate(flops=flops, bytes_accessed=moved, transcendentals=0)


def in_hbm(value):
    return pltpu.with_memory_space_constraint(value, pltpu.HBM)


def in_vmem(value):
    return pltpu.with_memory_space_constraint(value, pltpu.VMEM)


def spans(model):
    step = model // sum(CHUNKS)
    starts = [sum(CHUNKS[:c]) * step for c in range(len(CHUNKS))]
    return [(start, size * step) for start, size in zip(starts, CHUNKS)]


def whole(count):
    return [pl.BlockSpec(memory_space=pltpu.VMEM)] * count


def pack_kernel(section_ref, ids_in, probs_in, tokens_in, info_ref, packed_ref, ids_ref, probs_ref, tokens_ref, sems):
    pairs = ((ids_in, ids_ref), (probs_in, probs_ref), (tokens_in, tokens_ref))
    copies = [pltpu.make_async_copy(a, b, sems.at[i]) for i, (a, b) in enumerate(pairs)]
    for copy in copies:
        copy.start()
    copies[0].wait()
    copies[1].wait()
    section = section_ref[0]
    hit = (ids_ref[...] == section).astype(jnp.float32)
    tokens_count = hit.shape[1]
    routed = jnp.max(hit, axis=0, keepdims=True)
    weight = jnp.sum(hit * probs_ref[...], axis=0, keepdims=True)
    row = lax.broadcasted_iota(jnp.int32, (tokens_count, tokens_count), 0)
    col = lax.broadcasted_iota(jnp.int32, (tokens_count, tokens_count), 1)
    before = (row <= col).astype(jnp.bfloat16)
    counted = jnp.dot(
        jnp.broadcast_to(routed, (MAIN, tokens_count)).astype(jnp.bfloat16),
        before,
        preferred_element_type=jnp.float32,
    )[:1]
    slot = jnp.where(routed > 0.0, counted - 1.0, -1.0)
    out_row = lax.broadcasted_iota(jnp.int32, (2 * MAIN, tokens_count), 0)
    wanted = jnp.where(out_row < MAIN, out_row, MAIN + (out_row - MAIN) // SLABS)
    placed = slot == wanted.astype(jnp.float32)
    width = tokens_ref.shape[1]
    slab = width // SLABS
    copies[2].wait()
    rest = jnp.zeros((MAIN, slab), jnp.float32)
    for k in range(SLABS):
        keep = placed & ((out_row < MAIN) | (out_row % SLABS == k))
        mark = jnp.where(keep, 1.0, 0.0).astype(jnp.bfloat16)
        part = slice(k * slab, (k + 1) * slab)
        got = jnp.dot(mark, tokens_ref[:, part], preferred_element_type=jnp.float32)
        packed_ref[:, part] = got[:MAIN].astype(jnp.bfloat16)
        rest = rest + got[MAIN:]
    packed_ref[:, width:] = rest.astype(jnp.bfloat16)
    high = weight.astype(jnp.bfloat16).astype(jnp.float32)
    middle = (weight - high).astype(jnp.bfloat16).astype(jnp.float32)
    low = weight - high - middle
    kind = lax.broadcasted_iota(jnp.int32, (128, tokens_count), 0) % 8
    values = jnp.where(kind == 0, slot, jnp.where(kind == 1, high, jnp.where(kind == 2, middle, low)))
    values = jnp.where(kind < 4, values, 0.0).T
    token = lax.broadcasted_iota(jnp.int32, (tokens_count, 128), 0)
    lane = lax.broadcasted_iota(jnp.int32, (tokens_count, 128), 1)
    values = jnp.where(lane // 8 == token // MAIN, values, 0.0).astype(jnp.bfloat16)
    fold_row = lax.broadcasted_iota(jnp.int32, (MAIN, tokens_count), 0)
    fold_col = lax.broadcasted_iota(jnp.int32, (MAIN, tokens_count), 1)
    fold = (fold_col % MAIN == fold_row).astype(jnp.bfloat16)
    info_ref[...] = jnp.dot(fold, values, preferred_element_type=jnp.float32).astype(jnp.bfloat16)


def fetch_kernel(after_ref, *refs):
    done_ref, sems = refs[-2:]
    done_ref[...] = jnp.zeros(done_ref.shape, done_ref.dtype)
    copies = []
    for a, (source, target) in enumerate(zip(refs[:3], refs[3:])):
        step = source.shape[0] // 8
        for i in range(8):
            part = pl.ds(i * step, step)
            copies.append(pltpu.make_async_copy(source.at[part], target.at[part], sems.at[a, i]))
    for copy in copies:
        copy.start()
    for copy in copies:
        copy.wait()


def regroup(blocks, back):
    size = blocks * 2 * SLABS
    r = lax.broadcasted_iota(jnp.int32, (size, size), 1 if back else 0)
    q = lax.broadcasted_iota(jnp.int32, (size, size), 0 if back else 1)
    slab, pair = r // (2 * blocks), r % (2 * blocks)
    return (q == pair * SLABS + slab).astype(jnp.bfloat16)


def gather_rows(blocks, block_refs, x_ref):
    width = x_ref.shape[1]
    slab = width // SLABS
    row = 0
    for ref in block_refs:
        x_ref[row : row + ref.shape[0], :] = ref[:, :width]
        row += ref.shape[0]
    rest = jnp.concatenate([ref[:, width:] for ref in block_refs], axis=0)
    rest = jnp.dot(regroup(blocks, False), rest, preferred_element_type=jnp.float32).astype(jnp.bfloat16)
    for k in range(SLABS):
        x_ref[blocks * MAIN :, k * slab : (k + 1) * slab] = rest[k * 2 * blocks : (k + 1) * 2 * blocks]


def stack_kernel(blocks, *refs):
    out_ref = refs[-1]
    for b, ref in enumerate(refs[:blocks]):
        out_ref[b * MAIN : (b + 1) * MAIN, :] = ref[...]


def hidden_kernel(blocks, w_gate_ref, w_up_ref, *refs):
    block_refs, (hidden_ref, x_ref) = refs[:-2], refs[-2:]
    gather_rows(blocks, block_refs, x_ref)
    gate = jnp.dot(x_ref[...], w_gate_ref[...], preferred_element_type=jnp.float32)
    upper = jnp.dot(x_ref[...], w_up_ref[...], preferred_element_type=jnp.float32)
    hidden_ref[...] = (gate / (1.0 + jnp.exp(-gate)) * upper).astype(jnp.bfloat16)


def down_kernel(blocks, chunk, hidden_ref, w_down_ref, own_ref, other_ref):
    half = blocks // 2 * MAIN
    start, width = spans(w_down_ref.shape[1])[chunk]
    slab = width // SLABS
    part = slice(start, start + width)
    got = jnp.dot(hidden_ref[...], w_down_ref[:, part], preferred_element_type=jnp.float32)
    main = blocks * MAIN
    own_ref[:, :width] = got[:half].astype(own_ref.dtype)
    other_ref[:, :width] = got[half:main].astype(jnp.bfloat16)
    rest = got[main:].astype(jnp.bfloat16)
    stacked = jnp.concatenate([rest[:, k * slab : (k + 1) * slab] for k in range(SLABS)], axis=0)
    rest = jnp.dot(regroup(blocks, True), stacked, preferred_element_type=jnp.float32)
    own_ref[:, width:] = rest[:half].astype(own_ref.dtype)
    other_ref[:, width:] = rest[half:].astype(jnp.bfloat16)


def add_kernel(own_ref, other_ref, *out_refs):
    total = own_ref[...].astype(jnp.float32) + other_ref[...].astype(jnp.float32)
    for m, ref in enumerate(out_refs):
        ref[...] = total[m * MAIN : (m + 1) * MAIN].astype(ref.dtype)


def sum_kernel(parts, *refs):
    out_ref = refs[-1]
    total = refs[0][...]
    for ref in refs[1:parts]:
        total = total + ref[...].astype(jnp.float32)
    width = total.shape[1]
    out_ref[:, :width] = total.astype(jnp.bfloat16)
    if len(refs) > parts + 1:
        out_ref[:, width:] = refs[parts][...]


def place_kernel(received_ref, place_ref):
    token = lax.broadcasted_iota(jnp.int32, (place_ref.shape[0], MAIN), 0)
    column = lax.broadcasted_iota(jnp.int32, (place_ref.shape[0], MAIN), 1)
    unfold = (token % MAIN == column).astype(jnp.bfloat16)
    wide = received_ref.shape[1] - 128
    info = jnp.dot(unfold, received_ref[:, wide:], preferred_element_type=jnp.float32)
    token = lax.broadcasted_iota(jnp.int32, info.shape, 0)
    lane = lax.broadcasted_iota(jnp.int32, info.shape, 1)
    info = jnp.where(lane // 8 == token // MAIN, info, 0.0)
    slot = jnp.sum(jnp.where(lane % 8 == 0, info, 0.0), axis=1, keepdims=True)
    weight = jnp.sum(jnp.where(lane % 8 == 0, 0.0, info), axis=1, keepdims=True)
    wanted = jnp.where(lane < MAIN, lane, MAIN + (lane - MAIN) // SLABS)
    placed = (slot == wanted.astype(jnp.float32)) & (lane < 2 * MAIN)
    place_ref[...] = jnp.where(placed, weight, 0.0)


def combine_kernel(chunks, *refs):
    out_ref = refs[-1]
    rows_ref, place_ref = refs[:2]
    place = place_ref[...]
    lane = lax.broadcasted_iota(jnp.int32, place.shape, 1)
    weight = jnp.max(place, axis=1, keepdims=True)
    model = rows_ref.shape[1]
    for k in range(SLABS):
        keep = (place > 0.0) & ((lane < MAIN) | (lane % SLABS == k))
        mark = jnp.where(keep, 1.0, 0.0).astype(jnp.bfloat16)[:, : 2 * MAIN]
        for i, c in enumerate(chunks):
            ref = refs[2 + i]
            start, width = spans(model)[c]
            slab = width // SLABS
            values = jnp.concatenate(
                [ref[:, k * slab : (k + 1) * slab], ref[:, width : width + slab]], axis=0
            )
            moved = jnp.dot(mark, values, preferred_element_type=jnp.float32)
            span = slice(start + k * slab, start + (k + 1) * slab)
            out_ref[:, span] = (rows_ref[:, span].astype(jnp.float32) + weight * moved).astype(jnp.bfloat16)


def on_device(rows, expert_ids, gate_probs, w_gate, w_up, w_down):
    bf16, f32 = jnp.bfloat16, jnp.float32
    _, count, model = rows.shape
    hidden_units = w_gate.shape[2]
    shards = lax.axis_size("shard")
    sections = lax.axis_size("section")
    chips = shards // 2
    wides = [width + width // SLABS for start, width in spans(model)]
    total_rows = shards * CAP

    def along(value, steps):
        return lax.ppermute(value, "shard", [(i, (i + 2 * steps) % shards) for i in range(shards)])

    def swap(value):
        return lax.ppermute(value, "shard", [(i, i ^ 1) for i in range(shards)])

    def onward(value):
        return lax.ppermute(value, "section", [(s, (s + 1) % sections) for s in range(sections)])

    section = lax.axis_index("section").astype(jnp.int32).reshape(1)
    info, packed = pl.pallas_call(
        pack_kernel,
        out_shape=[
            jax.ShapeDtypeStruct((MAIN, 128), bf16),
            jax.ShapeDtypeStruct((MAIN, model + model // SLABS), bf16),
        ],
        in_specs=[pl.BlockSpec(memory_space=pltpu.SMEM)] + [pl.BlockSpec(memory_space=pltpu.HBM)] * 3,
        out_specs=whole(2),
        scratch_shapes=[
            pltpu.VMEM(expert_ids.shape[:0:-1], jnp.int32),
            pltpu.VMEM(gate_probs.shape[:0:-1], f32),
            pltpu.VMEM((count, model), bf16),
            pltpu.SemaphoreType.DMA((3,)),
        ],
        compiler_params=params(),
        cost_estimate=cost(0, 4 * count * model),
        name="pack",
    )(section, in_hbm(expert_ids[0].T), in_hbm(gate_probs[0].T), in_hbm(rows[0]))

    mine = [packed] + [along(packed, m) for m in range(1, chips)]

    gate_w, up_w, down_w, done = pl.pallas_call(
        fetch_kernel,
        out_shape=[
            pltpu.VMEM((model, hidden_units), bf16),
            pltpu.VMEM((model, hidden_units), bf16),
            pltpu.VMEM((hidden_units, model), bf16),
            jax.ShapeDtypeStruct((8, 128), f32),
        ],
        in_specs=[pl.BlockSpec(memory_space=pl.ANY)] + [pl.BlockSpec(memory_space=pltpu.HBM)] * 3,
        out_specs=whole(4),
        scratch_shapes=[pltpu.SemaphoreType.DMA((3, 8))],
        compiler_params=pltpu.CompilerParams(vmem_limit_bytes=12*1024*1024),
        cost_estimate=cost(0, 3 * 2 * 2 * model * hidden_units),
        name="fetch",
    )(packed, in_hbm(w_gate[0]), in_hbm(w_up[0]), in_hbm(w_down[0]))
    rows_in = onward(rows[0])

    def stack(*blocks):
        return pl.pallas_call(
            lambda *refs: stack_kernel(len(blocks), *refs),
            out_shape=jax.ShapeDtypeStruct((len(blocks) * MAIN, model + model // SLABS), bf16),
            in_specs=whole(len(blocks)) + [pl.BlockSpec(memory_space=pl.ANY)],
            out_specs=pl.BlockSpec(memory_space=pltpu.VMEM),
            compiler_params=params(),
            name="stack",
        )(*blocks, done)

    held = [stack(*mine[: chips // 2]), stack(*mine[chips // 2 :])]
    hidden = pl.pallas_call(
        lambda *refs: hidden_kernel(shards, *refs),
        out_shape=jax.ShapeDtypeStruct((total_rows, hidden_units), bf16),
        in_specs=whole(6),
        out_specs=pl.BlockSpec(memory_space=pltpu.VMEM),
        scratch_shapes=[pltpu.VMEM((total_rows, model), bf16)],
        compiler_params=params(),
        cost_estimate=cost(4 * total_rows * model * hidden_units, 4 * model * hidden_units),
        name="hidden",
    )(gate_w, up_w, *held, *[swap(part) for part in held])

    halves = []
    for c, wide in enumerate(wides):
        own, other = pl.pallas_call(
            lambda *refs, c=c: down_kernel(shards, c, *refs),
            out_shape=[
                jax.ShapeDtypeStruct((chips * MAIN, wide), f32),
                jax.ShapeDtypeStruct((chips * MAIN, wide), bf16),
            ],
            in_specs=whole(2),
            out_specs=whole(2),
            compiler_params=params(),
            name="down",
        )(hidden, down_w)
        halves.append((own, swap(other)))
    arrived = []
    for c, (wide, (own, other)) in enumerate(zip(wides, halves)):
        kept, *leaving = pl.pallas_call(
            add_kernel,
            out_shape=[jax.ShapeDtypeStruct((MAIN, wide), f32)]
            + [jax.ShapeDtypeStruct((MAIN, wide), bf16)] * (chips - 1),
            in_specs=whole(2),
            out_specs=whole(chips),
            compiler_params=params(),
            name="add_cores",
        )(own, other)
        coming = [along(block, -m) for m, block in enumerate(leaving, 1)]
        extra = [info] if c == 0 else []
        summed = pl.pallas_call(
            lambda *refs: sum_kernel(chips, *refs),
            out_shape=jax.ShapeDtypeStruct((MAIN, wide + 128 * len(extra)), bf16),
            in_specs=whole(chips + len(extra)),
            out_specs=pl.BlockSpec(memory_space=pltpu.VMEM),
            compiler_params=params(),
            name="sum_chips",
        )(kept, *coming, *extra)
        arrived.append(onward(summed))
    place = pl.pallas_call(
        place_kernel,
        out_shape=jax.ShapeDtypeStruct((count, 128), f32),
        in_specs=whole(1),
        out_specs=pl.BlockSpec(memory_space=pltpu.VMEM),
        compiler_params=params(),
        name="place",
    )(arrived[0])
    out = pl.pallas_call(
        lambda *refs: combine_kernel(range(len(CHUNKS)), *refs),
        out_shape=jax.ShapeDtypeStruct((count, model), bf16),
        in_specs=whole(2 + len(CHUNKS)),
        out_specs=pl.BlockSpec(memory_space=pltpu.VMEM),
        compiler_params=params(),
        name="combine",
    )(rows_in, place, *arrived)
    return out[None]


def solution(mesh):
    in_specs = (
        P("section", "shard", None),
        P("section", "shard", None),
        P("section", "shard", None),
        P("section", None, "shard"),
        P("section", None, "shard"),
        P("section", "shard", None),
    )
    return jax.shard_map(
        on_device, mesh=mesh, in_specs=in_specs, out_specs=P("section", "shard", None), check_vma=False
    )
```

```python
import jax
import jax.numpy as jnp
from jax import lax
from jax.experimental import pallas as pl
from jax.experimental.pallas import tpu as pltpu
from jax.sharding import PartitionSpec as P

CAP = 18
MAIN = 16
SLABS = 8
CHUNKS = (3, 3)
VMEM_LIMIT = 8 * 1024 * 1024


def params():
    return pltpu.CompilerParams(vmem_limit_bytes=VMEM_LIMIT)


def cost(flops, moved):
    return pl.CostEstimate(flops=flops, bytes_accessed=moved, transcendentals=0)


def in_hbm(value):
    return pltpu.with_memory_space_constraint(value, pltpu.HBM)


def in_vmem(value):
    return pltpu.with_memory_space_constraint(value, pltpu.VMEM)


def spans(model):
    step = model // sum(CHUNKS)
    starts = [sum(CHUNKS[:c]) * step for c in range(len(CHUNKS))]
    return [(start, size * step) for start, size in zip(starts, CHUNKS)]


def whole(count):
    return [pl.BlockSpec(memory_space=pltpu.VMEM)] * count


def pack_kernel(section_ref, ids_in, probs_in, tokens_in, info_ref, packed_ref, ids_ref, probs_ref, tokens_ref, sems):
    pairs = ((ids_in, ids_ref), (probs_in, probs_ref), (tokens_in, tokens_ref))
    copies = [pltpu.make_async_copy(a, b, sems.at[i]) for i, (a, b) in enumerate(pairs)]
    for copy in copies:
        copy.start()
    copies[0].wait()
    copies[1].wait()
    section = section_ref[0]
    hit = (ids_ref[...] == section).astype(jnp.float32)
    tokens_count = hit.shape[1]
    routed = jnp.max(hit, axis=0, keepdims=True)
    weight = jnp.sum(hit * probs_ref[...], axis=0, keepdims=True)
    row = lax.broadcasted_iota(jnp.int32, (tokens_count, tokens_count), 0)
    col = lax.broadcasted_iota(jnp.int32, (tokens_count, tokens_count), 1)
    before = (row <= col).astype(jnp.bfloat16)
    counted = jnp.dot(
        jnp.broadcast_to(routed, (MAIN, tokens_count)).astype(jnp.bfloat16),
        before,
        preferred_element_type=jnp.float32,
    )[:1]
    slot = jnp.where(routed > 0.0, counted - 1.0, -1.0)
    out_row = lax.broadcasted_iota(jnp.int32, (2 * MAIN, tokens_count), 0)
    wanted = jnp.where(out_row < MAIN, out_row, MAIN + (out_row - MAIN) // SLABS)
    placed = slot == wanted.astype(jnp.float32)
    width = tokens_ref.shape[1]
    slab = width // SLABS
    copies[2].wait()
    rest = jnp.zeros((MAIN, slab), jnp.float32)
    for k in range(SLABS):
        keep = placed & ((out_row < MAIN) | (out_row % SLABS == k))
        mark = jnp.where(keep, 1.0, 0.0).astype(jnp.bfloat16)
        part = slice(k * slab, (k + 1) * slab)
        got = jnp.dot(mark, tokens_ref[:, part], preferred_element_type=jnp.float32)
        packed_ref[:, part] = got[:MAIN].astype(jnp.bfloat16)
        rest = rest + got[MAIN:]
    packed_ref[:, width:] = rest.astype(jnp.bfloat16)
    high = weight.astype(jnp.bfloat16).astype(jnp.float32)
    middle = (weight - high).astype(jnp.bfloat16).astype(jnp.float32)
    low = weight - high - middle
    kind = lax.broadcasted_iota(jnp.int32, (128, tokens_count), 0) % 8
    values = jnp.where(kind == 0, slot, jnp.where(kind == 1, high, jnp.where(kind == 2, middle, low)))
    values = jnp.where(kind < 4, values, 0.0).T
    token = lax.broadcasted_iota(jnp.int32, (tokens_count, 128), 0)
    lane = lax.broadcasted_iota(jnp.int32, (tokens_count, 128), 1)
    values = jnp.where(lane // 8 == token // MAIN, values, 0.0).astype(jnp.bfloat16)
    fold_row = lax.broadcasted_iota(jnp.int32, (MAIN, tokens_count), 0)
    fold_col = lax.broadcasted_iota(jnp.int32, (MAIN, tokens_count), 1)
    fold = (fold_col % MAIN == fold_row).astype(jnp.bfloat16)
    info_ref[...] = jnp.dot(fold, values, preferred_element_type=jnp.float32).astype(jnp.bfloat16)


def fetch_kernel(after_ref, *refs):
    done_ref, sems = refs[-2:]
    done_ref[...] = jnp.zeros(done_ref.shape, done_ref.dtype)
    copies = []
    for a, (source, target) in enumerate(zip(refs[:3], refs[3:])):
        step = source.shape[0] // 8
        for i in range(8):
            part = pl.ds(i * step, step)
            copies.append(pltpu.make_async_copy(source.at[part], target.at[part], sems.at[a, i]))
    for copy in copies:
        copy.start()
    for copy in copies:
        copy.wait()


def regroup(blocks, back):
    size = blocks * 2 * SLABS
    r = lax.broadcasted_iota(jnp.int32, (size, size), 1 if back else 0)
    q = lax.broadcasted_iota(jnp.int32, (size, size), 0 if back else 1)
    slab, pair = r // (2 * blocks), r % (2 * blocks)
    return (q == pair * SLABS + slab).astype(jnp.bfloat16)


def gather_rows(blocks, block_refs, x_ref):
    width = x_ref.shape[1]
    slab = width // SLABS
    row = 0
    for ref in block_refs:
        x_ref[row : row + ref.shape[0], :] = ref[:, :width]
        row += ref.shape[0]
    rest = jnp.concatenate([ref[:, width:] for ref in block_refs], axis=0)
    rest = jnp.dot(regroup(blocks, False), rest, preferred_element_type=jnp.float32).astype(jnp.bfloat16)
    for k in range(SLABS):
        x_ref[blocks * MAIN :, k * slab : (k + 1) * slab] = rest[k * 2 * blocks : (k + 1) * 2 * blocks]


def stack_kernel(blocks, *refs):
    out_ref = refs[-1]
    for b, ref in enumerate(refs[:blocks]):
        out_ref[b * MAIN : (b + 1) * MAIN, :] = ref[...]


def hidden_kernel(blocks, w_gate_ref, w_up_ref, *refs):
    block_refs, (hidden_ref, x_ref) = refs[:-2], refs[-2:]
    gather_rows(blocks, block_refs, x_ref)
    gate = jnp.dot(x_ref[...], w_gate_ref[...], preferred_element_type=jnp.float32)
    upper = jnp.dot(x_ref[...], w_up_ref[...], preferred_element_type=jnp.float32)
    hidden_ref[...] = (gate / (1.0 + jnp.exp(-gate)) * upper).astype(jnp.bfloat16)


def down_kernel(blocks, chunk, hidden_ref, w_down_ref, own_ref, other_ref):
    half = blocks // 2 * MAIN
    start, width = spans(w_down_ref.shape[1])[chunk]
    slab = width // SLABS
    part = slice(start, start + width)
    got = jnp.dot(hidden_ref[...], w_down_ref[:, part], preferred_element_type=jnp.float32)
    main = blocks * MAIN
    own_ref[:, :width] = got[:half].astype(own_ref.dtype)
    other_ref[:, :width] = got[half:main].astype(jnp.bfloat16)
    rest = got[main:].astype(jnp.bfloat16)
    stacked = jnp.concatenate([rest[:, k * slab : (k + 1) * slab] for k in range(SLABS)], axis=0)
    rest = jnp.dot(regroup(blocks, True), stacked, preferred_element_type=jnp.float32)
    own_ref[:, width:] = rest[:half].astype(own_ref.dtype)
    other_ref[:, width:] = rest[half:].astype(jnp.bfloat16)


def add_kernel(own_ref, other_ref, info_ref, *out_refs):
    total = own_ref[...].astype(jnp.float32) + other_ref[...].astype(jnp.float32)
    wide = total.shape[1]
    for m, ref in enumerate(out_refs):
        ref[:, :wide] = total[m * MAIN : (m + 1) * MAIN].astype(ref.dtype)
        if ref.shape[1] > wide:
            ref[:, wide:] = info_ref[...]


def sum_kernel(parts, *refs):
    out_ref = refs[-1]
    total = refs[0][...]
    for ref in refs[1:parts]:
        total = total + ref[...].astype(jnp.float32)
    width = total.shape[1]
    out_ref[:, :width] = total.astype(jnp.bfloat16)
    if len(refs) > parts + 1:
        out_ref[:, width:] = refs[parts][...]


def combine_kernel(rows_ref, *refs):
    first_refs, last_refs, out_ref = refs[: len(CHUNKS) - 1], refs[len(CHUNKS) - 1 : -1], refs[-1]
    count, model = rows_ref.shape
    token = lax.broadcasted_iota(jnp.int32, (count, MAIN), 0)
    column = lax.broadcasted_iota(jnp.int32, (count, MAIN), 1)
    unfold = (token % MAIN == column).astype(jnp.bfloat16)
    wide = last_refs[0].shape[1] - 128
    info = jnp.dot(unfold, last_refs[0][:, wide:], preferred_element_type=jnp.float32)
    token = lax.broadcasted_iota(jnp.int32, info.shape, 0)
    lane = lax.broadcasted_iota(jnp.int32, info.shape, 1)
    info = jnp.where(lane // 8 == token // MAIN, info, 0.0)
    slot = jnp.sum(jnp.where(lane % 8 == 0, info, 0.0), axis=1, keepdims=True)
    weight = jnp.sum(jnp.where(lane % 8 == 0, 0.0, info), axis=1, keepdims=True)
    wanted = jnp.where(lane < MAIN, lane, MAIN + (lane - MAIN) // SLABS)
    placed = (slot == wanted.astype(jnp.float32)) & (lane < 2 * MAIN)
    total = jnp.zeros((MAIN, wide), jnp.float32)
    for ref in last_refs:
        total = total + ref[:, :wide].astype(jnp.float32)
    sums = [*first_refs, total.astype(jnp.bfloat16)]
    for k in range(SLABS):
        keep = placed & ((lane < MAIN) | (lane % SLABS == k))
        mark = jnp.where(keep, 1.0, 0.0).astype(jnp.bfloat16)[:, : 2 * MAIN]
        for ref, (start, width) in zip(sums, spans(model)):
            slab = width // SLABS
            values = jnp.concatenate(
                [ref[:, k * slab : (k + 1) * slab], ref[:, width : width + slab]], axis=0
            )
            moved = jnp.dot(mark, values, preferred_element_type=jnp.float32)
            span = slice(start + k * slab, start + (k + 1) * slab)
            out_ref[:, span] = (rows_ref[:, span].astype(jnp.float32) + weight * moved).astype(jnp.bfloat16)


def on_device(rows, expert_ids, gate_probs, w_gate, w_up, w_down):
    bf16, f32 = jnp.bfloat16, jnp.float32
    _, count, model = rows.shape
    hidden_units = w_gate.shape[2]
    shards = lax.axis_size("shard")
    sections = lax.axis_size("section")
    chips = shards // 2
    wides = [width + width // SLABS for start, width in spans(model)]
    total_rows = shards * CAP

    def across(value, steps):
        pairs = [
            (s * shards + i, (s + 1) % sections * shards + (i + 2 * steps) % shards)
            for s in range(sections)
            for i in range(shards)
        ]
        return lax.ppermute(value, ("section", "shard"), pairs)

    def along(value, steps):
        return lax.ppermute(value, "shard", [(i, (i + 2 * steps) % shards) for i in range(shards)])

    def swap(value):
        return lax.ppermute(value, "shard", [(i, i ^ 1) for i in range(shards)])

    def onward(value):
        return lax.ppermute(value, "section", [(s, (s + 1) % sections) for s in range(sections)])

    section = lax.axis_index("section").astype(jnp.int32).reshape(1)
    info, packed = pl.pallas_call(
        pack_kernel,
        out_shape=[
            jax.ShapeDtypeStruct((MAIN, 128), bf16),
            jax.ShapeDtypeStruct((MAIN, model + model // SLABS), bf16),
        ],
        in_specs=[pl.BlockSpec(memory_space=pltpu.SMEM)] + [pl.BlockSpec(memory_space=pltpu.HBM)] * 3,
        out_specs=whole(2),
        scratch_shapes=[
            pltpu.VMEM(expert_ids.shape[:0:-1], jnp.int32),
            pltpu.VMEM(gate_probs.shape[:0:-1], f32),
            pltpu.VMEM((count, model), bf16),
            pltpu.SemaphoreType.DMA((3,)),
        ],
        compiler_params=params(),
        cost_estimate=cost(0, 4 * count * model),
        name="pack",
    )(section, in_hbm(expert_ids[0].T), in_hbm(gate_probs[0].T), in_hbm(rows[0]))

    mine = [packed] + [along(packed, m) for m in range(1, chips)]

    gate_w, up_w, down_w, done = pl.pallas_call(
        fetch_kernel,
        out_shape=[
            pltpu.VMEM((model, hidden_units), bf16),
            pltpu.VMEM((model, hidden_units), bf16),
            pltpu.VMEM((hidden_units, model), bf16),
            jax.ShapeDtypeStruct((8, 128), f32),
        ],
        in_specs=[pl.BlockSpec(memory_space=pl.ANY)] + [pl.BlockSpec(memory_space=pltpu.HBM)] * 3,
        out_specs=whole(4),
        scratch_shapes=[pltpu.SemaphoreType.DMA((3, 8))],
        compiler_params=pltpu.CompilerParams(vmem_limit_bytes=12*1024*1024),
        cost_estimate=cost(0, 3 * 2 * 2 * model * hidden_units),
        name="fetch",
    )(packed, in_hbm(w_gate[0]), in_hbm(w_up[0]), in_hbm(w_down[0]))
    rows_in = onward(rows[0])

    def stack(*blocks):
        return pl.pallas_call(
            lambda *refs: stack_kernel(len(blocks), *refs),
            out_shape=jax.ShapeDtypeStruct((len(blocks) * MAIN, model + model // SLABS), bf16),
            in_specs=whole(len(blocks)) + [pl.BlockSpec(memory_space=pl.ANY)],
            out_specs=pl.BlockSpec(memory_space=pltpu.VMEM),
            compiler_params=params(),
            name="stack",
        )(*blocks, done)

    held = [stack(*mine[: chips // 2]), stack(*mine[chips // 2 :])]
    hidden = pl.pallas_call(
        lambda *refs: hidden_kernel(shards, *refs),
        out_shape=jax.ShapeDtypeStruct((total_rows, hidden_units), bf16),
        in_specs=whole(6),
        out_specs=pl.BlockSpec(memory_space=pltpu.VMEM),
        scratch_shapes=[pltpu.VMEM((total_rows, model), bf16)],
        compiler_params=params(),
        cost_estimate=cost(4 * total_rows * model * hidden_units, 4 * model * hidden_units),
        name="hidden",
    )(gate_w, up_w, *held, *[swap(part) for part in held])

    halves = []
    for c, wide in enumerate(wides):
        own, other = pl.pallas_call(
            lambda *refs, c=c: down_kernel(shards, c, *refs),
            out_shape=[
                jax.ShapeDtypeStruct((chips * MAIN, wide), f32),
                jax.ShapeDtypeStruct((chips * MAIN, wide), bf16),
            ],
            in_specs=whole(2),
            out_specs=whole(2),
            compiler_params=params(),
            name="down",
        )(hidden, down_w)
        halves.append((own, swap(other)))
    arrived = []
    for c, (wide, (own, other)) in enumerate(zip(wides, halves)):
        last = c == len(CHUNKS) - 1
        kept, *leaving = pl.pallas_call(
            add_kernel,
            out_shape=[jax.ShapeDtypeStruct((MAIN, wide + 128 * last), bf16 if last else f32)]
            + [jax.ShapeDtypeStruct((MAIN, wide + 128 * last), bf16)] * (chips - 1),
            in_specs=whole(3),
            out_specs=whole(chips),
            compiler_params=params(),
            name="add_cores",
        )(own, other, info)
        if last:
            arrived += [across(block, -m) for m, block in enumerate((kept, *leaving))]
            break
        coming = [along(block, -m) for m, block in enumerate(leaving, 1)]
        extra = []
        summed = pl.pallas_call(
            lambda *refs: sum_kernel(chips, *refs),
            out_shape=jax.ShapeDtypeStruct((MAIN, wide + 128 * len(extra)), bf16),
            in_specs=whole(chips + len(extra)),
            out_specs=pl.BlockSpec(memory_space=pltpu.VMEM),
            compiler_params=params(),
            name="sum_chips",
        )(kept, *coming, *extra)
        arrived.append(onward(summed))
    out = pl.pallas_call(
        combine_kernel,
        out_shape=jax.ShapeDtypeStruct((count, model), bf16),
        in_specs=whole(len(CHUNKS) + chips),
        out_specs=pl.BlockSpec(memory_space=pltpu.VMEM),
        compiler_params=params(),
        name="combine",
    )(rows_in, *arrived)
    return out[None]


def solution(mesh):
    in_specs = (
        P("section", "shard", None),
        P("section", "shard", None),
        P("section", "shard", None),
        P("section", None, "shard"),
        P("section", None, "shard"),
        P("section", "shard", None),
    )
    return jax.shard_map(
        on_device, mesh=mesh, in_specs=in_specs, out_specs=P("section", "shard", None), check_vma=False
    )
```

```python
import jax
import jax.numpy as jnp
from jax import lax
from jax.experimental import pallas as pl
from jax.experimental.pallas import tpu as pltpu
from jax.sharding import PartitionSpec as P

CAP = 18
MAIN = 16
SLABS = 8
CHUNKS = (3, 3)
VMEM_LIMIT = 8 * 1024 * 1024


def params():
    return pltpu.CompilerParams(vmem_limit_bytes=VMEM_LIMIT)


def cost(flops, moved):
    return pl.CostEstimate(flops=flops, bytes_accessed=moved, transcendentals=0)


def in_hbm(value):
    return pltpu.with_memory_space_constraint(value, pltpu.HBM)


def in_vmem(value):
    return pltpu.with_memory_space_constraint(value, pltpu.VMEM)


def spans(model):
    step = model // sum(CHUNKS)
    starts = [sum(CHUNKS[:c]) * step for c in range(len(CHUNKS))]
    return [(start, size * step) for start, size in zip(starts, CHUNKS)]


def whole(count):
    return [pl.BlockSpec(memory_space=pltpu.VMEM)] * count


def pack_kernel(section_ref, ids_in, probs_in, tokens_in, info_ref, packed_ref, ids_ref, probs_ref, tokens_ref, sems):
    pairs = ((ids_in, ids_ref), (probs_in, probs_ref), (tokens_in, tokens_ref))
    copies = [pltpu.make_async_copy(a, b, sems.at[i]) for i, (a, b) in enumerate(pairs)]
    for copy in copies:
        copy.start()
    copies[0].wait()
    copies[1].wait()
    section = section_ref[0]
    hit = (ids_ref[...] == section).astype(jnp.float32)
    tokens_count = hit.shape[1]
    routed = jnp.max(hit, axis=0, keepdims=True)
    weight = jnp.sum(hit * probs_ref[...], axis=0, keepdims=True)
    row = lax.broadcasted_iota(jnp.int32, (tokens_count, tokens_count), 0)
    col = lax.broadcasted_iota(jnp.int32, (tokens_count, tokens_count), 1)
    before = (row <= col).astype(jnp.bfloat16)
    counted = jnp.dot(
        jnp.broadcast_to(routed, (MAIN, tokens_count)).astype(jnp.bfloat16),
        before,
        preferred_element_type=jnp.float32,
    )[:1]
    slot = jnp.where(routed > 0.0, counted - 1.0, -1.0)
    out_row = lax.broadcasted_iota(jnp.int32, (2 * MAIN, tokens_count), 0)
    wanted = jnp.where(out_row < MAIN, out_row, MAIN + (out_row - MAIN) // SLABS)
    placed = slot == wanted.astype(jnp.float32)
    width = tokens_ref.shape[1]
    slab = width // SLABS
    copies[2].wait()
    rest = jnp.zeros((MAIN, slab), jnp.float32)
    for k in range(SLABS):
        keep = placed & ((out_row < MAIN) | (out_row % SLABS == k))
        mark = jnp.where(keep, 1.0, 0.0).astype(jnp.bfloat16)
        part = slice(k * slab, (k + 1) * slab)
        got = jnp.dot(mark, tokens_ref[:, part], preferred_element_type=jnp.float32)
        packed_ref[:, part] = got[:MAIN].astype(jnp.bfloat16)
        rest = rest + got[MAIN:]
    packed_ref[:, width:] = rest.astype(jnp.bfloat16)
    high = weight.astype(jnp.bfloat16).astype(jnp.float32)
    middle = (weight - high).astype(jnp.bfloat16).astype(jnp.float32)
    low = weight - high - middle
    kind = lax.broadcasted_iota(jnp.int32, (128, tokens_count), 0) % 8
    values = jnp.where(kind == 0, slot, jnp.where(kind == 1, high, jnp.where(kind == 2, middle, low)))
    values = jnp.where(kind < 4, values, 0.0).T
    token = lax.broadcasted_iota(jnp.int32, (tokens_count, 128), 0)
    lane = lax.broadcasted_iota(jnp.int32, (tokens_count, 128), 1)
    values = jnp.where(lane // 8 == token // MAIN, values, 0.0).astype(jnp.bfloat16)
    fold_row = lax.broadcasted_iota(jnp.int32, (MAIN, tokens_count), 0)
    fold_col = lax.broadcasted_iota(jnp.int32, (MAIN, tokens_count), 1)
    fold = (fold_col % MAIN == fold_row).astype(jnp.bfloat16)
    info_ref[...] = jnp.dot(fold, values, preferred_element_type=jnp.float32).astype(jnp.bfloat16)


def fetch_kernel(after_ref, *refs):
    done_ref, sems = refs[-2:]
    done_ref[...] = jnp.zeros(done_ref.shape, done_ref.dtype)
    copies = []
    for a, (source, target) in enumerate(zip(refs[:3], refs[3:])):
        step = source.shape[0] // 8
        for i in range(8):
            part = pl.ds(i * step, step)
            copies.append(pltpu.make_async_copy(source.at[part], target.at[part], sems.at[a, i]))
    for copy in copies:
        copy.start()
    for copy in copies:
        copy.wait()


def regroup(blocks, back):
    size = blocks * 2 * SLABS
    r = lax.broadcasted_iota(jnp.int32, (size, size), 1 if back else 0)
    q = lax.broadcasted_iota(jnp.int32, (size, size), 0 if back else 1)
    slab, pair = r // (2 * blocks), r % (2 * blocks)
    return (q == pair * SLABS + slab).astype(jnp.bfloat16)


def gather_rows(blocks, block_refs, x_ref):
    width = x_ref.shape[1]
    slab = width // SLABS
    row = 0
    for ref in block_refs:
        x_ref[row : row + ref.shape[0], :] = ref[:, :width]
        row += ref.shape[0]
    rest = jnp.concatenate([ref[:, width:] for ref in block_refs], axis=0)
    rest = jnp.dot(regroup(blocks, False), rest, preferred_element_type=jnp.float32).astype(jnp.bfloat16)
    for k in range(SLABS):
        x_ref[blocks * MAIN :, k * slab : (k + 1) * slab] = rest[k * 2 * blocks : (k + 1) * 2 * blocks]


def stack_kernel(blocks, *refs):
    out_ref = refs[-1]
    for b, ref in enumerate(refs[:blocks]):
        out_ref[b * MAIN : (b + 1) * MAIN, :] = ref[...]


def hidden_kernel(blocks, w_gate_ref, w_up_ref, *refs):
    block_refs, (hidden_ref, x_ref) = refs[:-2], refs[-2:]
    gather_rows(blocks, block_refs, x_ref)
    gate = jnp.dot(x_ref[...], w_gate_ref[...], preferred_element_type=jnp.float32)
    upper = jnp.dot(x_ref[...], w_up_ref[...], preferred_element_type=jnp.float32)
    hidden_ref[...] = (gate / (1.0 + jnp.exp(-gate)) * upper).astype(jnp.bfloat16)


def down_kernel(blocks, chunk, hidden_ref, w_down_ref, own_ref, other_ref):
    half = blocks // 2 * MAIN
    start, width = spans(w_down_ref.shape[1])[chunk]
    slab = width // SLABS
    part = slice(start, start + width)
    got = jnp.dot(hidden_ref[...], w_down_ref[:, part], preferred_element_type=jnp.float32)
    main = blocks * MAIN
    own_ref[:, :width] = got[:half].astype(own_ref.dtype)
    other_ref[:, :width] = got[half:main].astype(jnp.bfloat16)
    rest = got[main:].astype(jnp.bfloat16)
    stacked = jnp.concatenate([rest[:, k * slab : (k + 1) * slab] for k in range(SLABS)], axis=0)
    rest = jnp.dot(regroup(blocks, True), stacked, preferred_element_type=jnp.float32)
    own_ref[:, width:] = rest[:half].astype(own_ref.dtype)
    other_ref[:, width:] = rest[half:].astype(jnp.bfloat16)


def add_kernel(own_ref, other_ref, info_ref, *out_refs):
    total = own_ref[...].astype(jnp.float32) + other_ref[...].astype(jnp.float32)
    wide = total.shape[1]
    for m, ref in enumerate(out_refs):
        ref[:, :wide] = total[m * MAIN : (m + 1) * MAIN].astype(ref.dtype)
        if ref.shape[1] > wide:
            ref[:, wide:] = info_ref[...]


def sum_kernel(parts, *refs):
    out_ref = refs[-1]
    total = refs[0][...]
    for ref in refs[1:parts]:
        total = total + ref[...].astype(jnp.float32)
    width = total.shape[1]
    out_ref[:, :width] = total.astype(jnp.bfloat16)
    if len(refs) > parts + 1:
        out_ref[:, width:] = refs[parts][...]


def combine_kernel(rows_ref, *refs):
    first_refs, last_refs, out_ref = refs[: len(CHUNKS) - 1], refs[len(CHUNKS) - 1 : -1], refs[-1]
    count, model = rows_ref.shape
    token = lax.broadcasted_iota(jnp.int32, (count, MAIN), 0)
    column = lax.broadcasted_iota(jnp.int32, (count, MAIN), 1)
    unfold = (token % MAIN == column).astype(jnp.bfloat16)
    wide = last_refs[0].shape[1] - 128
    info = jnp.dot(unfold, last_refs[0][:, wide:], preferred_element_type=jnp.float32)
    token = lax.broadcasted_iota(jnp.int32, info.shape, 0)
    lane = lax.broadcasted_iota(jnp.int32, info.shape, 1)
    info = jnp.where(lane // 8 == token // MAIN, info, 0.0)
    slot = jnp.sum(jnp.where(lane % 8 == 0, info, 0.0), axis=1, keepdims=True)
    weight = jnp.sum(jnp.where(lane % 8 == 0, 0.0, info), axis=1, keepdims=True)
    wanted = jnp.where(lane < MAIN, lane, MAIN + (lane - MAIN) // SLABS)
    placed = (slot == wanted.astype(jnp.float32)) & (lane < 2 * MAIN)
    total = jnp.zeros((MAIN, wide), jnp.float32)
    for ref in last_refs:
        total = total + ref[:, :wide].astype(jnp.float32)
    sums = [*first_refs, total.astype(jnp.bfloat16)]
    for k in range(SLABS):
        keep = placed & ((lane < MAIN) | (lane % SLABS == k))
        mark = jnp.where(keep, 1.0, 0.0).astype(jnp.bfloat16)[:, : 2 * MAIN]
        for ref, (start, width) in zip(sums, spans(model)):
            slab = width // SLABS
            values = jnp.concatenate(
                [ref[:, k * slab : (k + 1) * slab], ref[:, width : width + slab]], axis=0
            )
            moved = jnp.dot(mark, values, preferred_element_type=jnp.float32)
            span = slice(start + k * slab, start + (k + 1) * slab)
            out_ref[:, span] = (rows_ref[:, span].astype(jnp.float32) + weight * moved).astype(jnp.bfloat16)


def on_device(rows, expert_ids, gate_probs, w_gate, w_up, w_down):
    bf16, f32 = jnp.bfloat16, jnp.float32
    _, count, model = rows.shape
    hidden_units = w_gate.shape[2]
    shards = lax.axis_size("shard")
    sections = lax.axis_size("section")
    chips = shards // 2
    wides = [width + width // SLABS for start, width in spans(model)]
    total_rows = shards * CAP

    def across(value, flip):
        pairs = [
            (s * shards + i, (s + 1) % sections * shards + (i ^ (2 * flip)))
            for s in range(sections)
            for i in range(shards)
        ]
        return lax.ppermute(value, ("section", "shard"), pairs)

    def along(value, flip):
        return lax.ppermute(value, "shard", [(i, i ^ (2 * flip)) for i in range(shards)])

    def swap(value):
        return lax.ppermute(value, "shard", [(i, i ^ 1) for i in range(shards)])

    def onward(value):
        return lax.ppermute(value, "section", [(s, (s + 1) % sections) for s in range(sections)])

    section = lax.axis_index("section").astype(jnp.int32).reshape(1)
    info, packed = pl.pallas_call(
        pack_kernel,
        out_shape=[
            jax.ShapeDtypeStruct((MAIN, 128), bf16),
            jax.ShapeDtypeStruct((MAIN, model + model // SLABS), bf16),
        ],
        in_specs=[pl.BlockSpec(memory_space=pltpu.SMEM)] + [pl.BlockSpec(memory_space=pltpu.HBM)] * 3,
        out_specs=whole(2),
        scratch_shapes=[
            pltpu.VMEM(expert_ids.shape[:0:-1], jnp.int32),
            pltpu.VMEM(gate_probs.shape[:0:-1], f32),
            pltpu.VMEM((count, model), bf16),
            pltpu.SemaphoreType.DMA((3,)),
        ],
        compiler_params=params(),
        cost_estimate=cost(0, 4 * count * model),
        name="pack",
    )(section, in_hbm(expert_ids[0].T), in_hbm(gate_probs[0].T), in_hbm(rows[0]))

    mine = [packed] + [along(packed, m) for m in range(1, chips)]

    gate_w, up_w, down_w, done = pl.pallas_call(
        fetch_kernel,
        out_shape=[
            pltpu.VMEM((model, hidden_units), bf16),
            pltpu.VMEM((model, hidden_units), bf16),
            pltpu.VMEM((hidden_units, model), bf16),
            jax.ShapeDtypeStruct((8, 128), f32),
        ],
        in_specs=[pl.BlockSpec(memory_space=pl.ANY)] + [pl.BlockSpec(memory_space=pltpu.HBM)] * 3,
        out_specs=whole(4),
        scratch_shapes=[pltpu.SemaphoreType.DMA((3, 8))],
        compiler_params=pltpu.CompilerParams(vmem_limit_bytes=12*1024*1024),
        cost_estimate=cost(0, 3 * 2 * 2 * model * hidden_units),
        name="fetch",
    )(packed, in_hbm(w_gate[0]), in_hbm(w_up[0]), in_hbm(w_down[0]))
    rows_in = onward(rows[0])

    def stack(*blocks):
        return pl.pallas_call(
            lambda *refs: stack_kernel(len(blocks), *refs),
            out_shape=jax.ShapeDtypeStruct((len(blocks) * MAIN, model + model // SLABS), bf16),
            in_specs=whole(len(blocks)) + [pl.BlockSpec(memory_space=pl.ANY)],
            out_specs=pl.BlockSpec(memory_space=pltpu.VMEM),
            compiler_params=params(),
            name="stack",
        )(*blocks, done)

    held = [stack(*mine[: chips // 2]), stack(*mine[chips // 2 :])]
    hidden = pl.pallas_call(
        lambda *refs: hidden_kernel(shards, *refs),
        out_shape=jax.ShapeDtypeStruct((total_rows, hidden_units), bf16),
        in_specs=whole(6),
        out_specs=pl.BlockSpec(memory_space=pltpu.VMEM),
        scratch_shapes=[pltpu.VMEM((total_rows, model), bf16)],
        compiler_params=params(),
        cost_estimate=cost(4 * total_rows * model * hidden_units, 4 * model * hidden_units),
        name="hidden",
    )(gate_w, up_w, *held, *[swap(part) for part in held])

    halves = []
    for c, wide in enumerate(wides):
        own, other = pl.pallas_call(
            lambda *refs, c=c: down_kernel(shards, c, *refs),
            out_shape=[
                jax.ShapeDtypeStruct((chips * MAIN, wide), f32),
                jax.ShapeDtypeStruct((chips * MAIN, wide), bf16),
            ],
            in_specs=whole(2),
            out_specs=whole(2),
            compiler_params=params(),
            name="down",
        )(hidden, down_w)
        halves.append((own, swap(other)))
    arrived = []
    for c, (wide, (own, other)) in enumerate(zip(wides, halves)):
        last = c == len(CHUNKS) - 1
        kept, *leaving = pl.pallas_call(
            add_kernel,
            out_shape=[jax.ShapeDtypeStruct((MAIN, wide + 128 * last), bf16 if last else f32)]
            + [jax.ShapeDtypeStruct((MAIN, wide + 128 * last), bf16)] * (chips - 1),
            in_specs=whole(3),
            out_specs=whole(chips),
            compiler_params=params(),
            name="add_cores",
        )(own, other, info)
        if last:
            arrived += [across(block, m) for m, block in enumerate((kept, *leaving))]
            break
        coming = [along(leaving[m - 1], m) for m in (chips - 1, *range(1, chips - 1))]
        extra = []
        summed = pl.pallas_call(
            lambda *refs: sum_kernel(chips, *refs),
            out_shape=jax.ShapeDtypeStruct((MAIN, wide + 128 * len(extra)), bf16),
            in_specs=whole(chips + len(extra)),
            out_specs=pl.BlockSpec(memory_space=pltpu.VMEM),
            compiler_params=params(),
            name="sum_chips",
        )(kept, *coming, *extra)
        arrived.append(onward(summed))
    out = pl.pallas_call(
        combine_kernel,
        out_shape=jax.ShapeDtypeStruct((count, model), bf16),
        in_specs=whole(len(CHUNKS) + chips),
        out_specs=pl.BlockSpec(memory_space=pltpu.VMEM),
        compiler_params=params(),
        name="combine",
    )(rows_in, *arrived)
    return out[None]


def solution(mesh):
    in_specs = (
        P("section", "shard", None),
        P("section", "shard", None),
        P("section", "shard", None),
        P("section", None, "shard"),
        P("section", None, "shard"),
        P("section", "shard", None),
    )
    return jax.shard_map(
        on_device, mesh=mesh, in_specs=in_specs, out_specs=P("section", "shard", None), check_vma=False
    )
```

```python
import jax
import jax.numpy as jnp
from jax import lax
from jax.experimental import pallas as pl
from jax.experimental.pallas import tpu as pltpu
from jax.sharding import PartitionSpec as P

CAP = 18
MAIN = 16
SLABS = 8
CHUNKS = (3, 3)
VMEM_LIMIT = 8 * 1024 * 1024


def params():
    return pltpu.CompilerParams(vmem_limit_bytes=VMEM_LIMIT)


def cost(flops, moved):
    return pl.CostEstimate(flops=flops, bytes_accessed=moved, transcendentals=0)


def in_hbm(value):
    return pltpu.with_memory_space_constraint(value, pltpu.HBM)


def in_vmem(value):
    return pltpu.with_memory_space_constraint(value, pltpu.VMEM)


def spans(model):
    step = model // sum(CHUNKS)
    starts = [sum(CHUNKS[:c]) * step for c in range(len(CHUNKS))]
    return [(start, size * step) for start, size in zip(starts, CHUNKS)]


def whole(count):
    return [pl.BlockSpec(memory_space=pltpu.VMEM)] * count


def pack_kernel(section_ref, ids_in, probs_in, tokens_in, info_ref, packed_ref, ids_ref, probs_ref, tokens_ref, sems):
    pairs = ((ids_in, ids_ref), (probs_in, probs_ref), (tokens_in, tokens_ref))
    copies = [pltpu.make_async_copy(a, b, sems.at[i]) for i, (a, b) in enumerate(pairs)]
    for copy in copies:
        copy.start()
    copies[0].wait()
    copies[1].wait()
    section = section_ref[0]
    hit = (ids_ref[...] == section).astype(jnp.float32)
    tokens_count = hit.shape[1]
    routed = jnp.max(hit, axis=0, keepdims=True)
    weight = jnp.sum(hit * probs_ref[...], axis=0, keepdims=True)
    row = lax.broadcasted_iota(jnp.int32, (tokens_count, tokens_count), 0)
    col = lax.broadcasted_iota(jnp.int32, (tokens_count, tokens_count), 1)
    before = (row <= col).astype(jnp.bfloat16)
    counted = jnp.dot(
        jnp.broadcast_to(routed, (MAIN, tokens_count)).astype(jnp.bfloat16),
        before,
        preferred_element_type=jnp.float32,
    )[:1]
    slot = jnp.where(routed > 0.0, counted - 1.0, -1.0)
    out_row = lax.broadcasted_iota(jnp.int32, (2 * MAIN, tokens_count), 0)
    wanted = jnp.where(out_row < MAIN, out_row, MAIN + (out_row - MAIN) // SLABS)
    placed = slot == wanted.astype(jnp.float32)
    width = tokens_ref.shape[1]
    slab = width // SLABS
    copies[2].wait()
    rest = jnp.zeros((MAIN, slab), jnp.float32)
    for k in range(SLABS):
        keep = placed & ((out_row < MAIN) | (out_row % SLABS == k))
        mark = jnp.where(keep, 1.0, 0.0).astype(jnp.bfloat16)
        part = slice(k * slab, (k + 1) * slab)
        got = jnp.dot(mark, tokens_ref[:, part], preferred_element_type=jnp.float32)
        packed_ref[:, part] = got[:MAIN].astype(jnp.bfloat16)
        rest = rest + got[MAIN:]
    packed_ref[:, width:] = rest.astype(jnp.bfloat16)
    high = weight.astype(jnp.bfloat16).astype(jnp.float32)
    middle = (weight - high).astype(jnp.bfloat16).astype(jnp.float32)
    low = weight - high - middle
    kind = lax.broadcasted_iota(jnp.int32, (128, tokens_count), 0) % 8
    values = jnp.where(kind == 0, slot, jnp.where(kind == 1, high, jnp.where(kind == 2, middle, low)))
    values = jnp.where(kind < 4, values, 0.0).T
    token = lax.broadcasted_iota(jnp.int32, (tokens_count, 128), 0)
    lane = lax.broadcasted_iota(jnp.int32, (tokens_count, 128), 1)
    values = jnp.where(lane // 8 == token // MAIN, values, 0.0).astype(jnp.bfloat16)
    fold_row = lax.broadcasted_iota(jnp.int32, (MAIN, tokens_count), 0)
    fold_col = lax.broadcasted_iota(jnp.int32, (MAIN, tokens_count), 1)
    fold = (fold_col % MAIN == fold_row).astype(jnp.bfloat16)
    info_ref[...] = jnp.dot(fold, values, preferred_element_type=jnp.float32).astype(jnp.bfloat16)


def fetch_kernel(after_ref, *refs):
    done_ref, sems = refs[-2:]
    done_ref[...] = jnp.zeros(done_ref.shape, done_ref.dtype)
    copies = []
    for a, (source, target) in enumerate(zip(refs[:3], refs[3:])):
        step = source.shape[0] // 8
        for i in range(8):
            part = pl.ds(i * step, step)
            copies.append(pltpu.make_async_copy(source.at[part], target.at[part], sems.at[a, i]))
    for copy in copies:
        copy.start()
    for copy in copies:
        copy.wait()


def regroup(blocks, back):
    size = blocks * 2 * SLABS
    r = lax.broadcasted_iota(jnp.int32, (size, size), 1 if back else 0)
    q = lax.broadcasted_iota(jnp.int32, (size, size), 0 if back else 1)
    slab, pair = r // (2 * blocks), r % (2 * blocks)
    return (q == pair * SLABS + slab).astype(jnp.bfloat16)


def gather_rows(blocks, block_refs, x_ref):
    width = x_ref.shape[1]
    slab = width // SLABS
    row = 0
    for ref in block_refs:
        x_ref[row : row + ref.shape[0], :] = ref[:, :width]
        row += ref.shape[0]
    rest = jnp.concatenate([ref[:, width:] for ref in block_refs], axis=0)
    rest = jnp.dot(regroup(blocks, False), rest, preferred_element_type=jnp.float32).astype(jnp.bfloat16)
    for k in range(SLABS):
        x_ref[blocks * MAIN :, k * slab : (k + 1) * slab] = rest[k * 2 * blocks : (k + 1) * 2 * blocks]


def stack_kernel(blocks, *refs):
    out_ref = refs[-1]
    for b, ref in enumerate(refs[:blocks]):
        out_ref[b * MAIN : (b + 1) * MAIN, :] = ref[...]


def hidden_kernel(blocks, w_gate_ref, w_up_ref, *refs):
    block_refs, (hidden_ref, x_ref) = refs[:-2], refs[-2:]
    gather_rows(blocks, block_refs, x_ref)
    gate = jnp.dot(x_ref[...], w_gate_ref[...], preferred_element_type=jnp.float32)
    upper = jnp.dot(x_ref[...], w_up_ref[...], preferred_element_type=jnp.float32)
    hidden_ref[...] = (gate / (1.0 + jnp.exp(-gate)) * upper).astype(jnp.bfloat16)


def down_kernel(blocks, chunk, hidden_ref, w_down_ref, own_ref, other_ref):
    half = blocks // 2 * MAIN
    start, width = spans(w_down_ref.shape[1])[chunk]
    slab = width // SLABS
    part = slice(start, start + width)
    got = jnp.dot(hidden_ref[...], w_down_ref[:, part], preferred_element_type=jnp.float32)
    main = blocks * MAIN
    own_ref[:, :width] = got[:half].astype(own_ref.dtype)
    other_ref[:, :width] = got[half:main].astype(jnp.bfloat16)
    rest = got[main:].astype(jnp.bfloat16)
    stacked = jnp.concatenate([rest[:, k * slab : (k + 1) * slab] for k in range(SLABS)], axis=0)
    rest = jnp.dot(regroup(blocks, True), stacked, preferred_element_type=jnp.float32)
    own_ref[:, width:] = rest[:half].astype(own_ref.dtype)
    other_ref[:, width:] = rest[half:].astype(jnp.bfloat16)


def add_kernel(own_ref, other_ref, info_ref, *out_refs):
    total = own_ref[...].astype(jnp.float32) + other_ref[...].astype(jnp.float32)
    wide = total.shape[1]
    for m, ref in enumerate(out_refs):
        ref[:, :wide] = total[m * MAIN : (m + 1) * MAIN].astype(ref.dtype)
        if ref.shape[1] > wide:
            ref[:, wide:] = info_ref[...]


def sum_kernel(parts, *refs):
    out_ref = refs[-1]
    total = refs[0][...]
    for ref in refs[1:parts]:
        total = total + ref[...].astype(jnp.float32)
    width = total.shape[1]
    out_ref[:, :width] = total.astype(jnp.bfloat16)
    if len(refs) > parts + 1:
        out_ref[:, width:] = refs[parts][...]


def combine_kernel(rows_ref, *refs):
    first_refs, last_refs, out_ref = refs[: len(CHUNKS) - 1], refs[len(CHUNKS) - 1 : -1], refs[-1]
    count, model = rows_ref.shape
    token = lax.broadcasted_iota(jnp.int32, (count, MAIN), 0)
    column = lax.broadcasted_iota(jnp.int32, (count, MAIN), 1)
    unfold = (token % MAIN == column).astype(jnp.bfloat16)
    wide = last_refs[0].shape[1] - 128
    info = jnp.dot(unfold, last_refs[0][:, wide:], preferred_element_type=jnp.float32)
    token = lax.broadcasted_iota(jnp.int32, info.shape, 0)
    lane = lax.broadcasted_iota(jnp.int32, info.shape, 1)
    info = jnp.where(lane // 8 == token // MAIN, info, 0.0)
    slot = jnp.sum(jnp.where(lane % 8 == 0, info, 0.0), axis=1, keepdims=True)
    weight = jnp.sum(jnp.where(lane % 8 == 0, 0.0, info), axis=1, keepdims=True)
    wanted = jnp.where(lane < MAIN, lane, MAIN + (lane - MAIN) // SLABS)
    placed = (slot == wanted.astype(jnp.float32)) & (lane < 2 * MAIN)
    total = jnp.zeros((MAIN, wide), jnp.float32)
    for ref in last_refs:
        total = total + ref[:, :wide].astype(jnp.float32)
    sums = [*first_refs, total.astype(jnp.bfloat16)]
    for k in range(SLABS):
        keep = placed & ((lane < MAIN) | (lane % SLABS == k))
        mark = jnp.where(keep, 1.0, 0.0).astype(jnp.bfloat16)[:, : 2 * MAIN]
        for ref, (start, width) in zip(sums, spans(model)):
            slab = width // SLABS
            values = jnp.concatenate(
                [ref[:, k * slab : (k + 1) * slab], ref[:, width : width + slab]], axis=0
            )
            moved = jnp.dot(mark, values, preferred_element_type=jnp.float32)
            span = slice(start + k * slab, start + (k + 1) * slab)
            out_ref[:, span] = (rows_ref[:, span].astype(jnp.float32) + weight * moved).astype(jnp.bfloat16)


def on_device(rows, expert_ids, gate_probs, w_gate, w_up, w_down):
    bf16, f32 = jnp.bfloat16, jnp.float32
    _, count, model = rows.shape
    hidden_units = w_gate.shape[2]
    shards = lax.axis_size("shard")
    sections = lax.axis_size("section")
    chips = shards // 2
    wides = [width + width // SLABS for start, width in spans(model)]
    total_rows = shards * CAP

    def across(value, flip):
        pairs = [
            (s * shards + i, (s + 1) % sections * shards + (i ^ (2 * flip)))
            for s in range(sections)
            for i in range(shards)
        ]
        return lax.ppermute(value, ("section", "shard"), pairs)

    def along(value, flip):
        return lax.ppermute(value, "shard", [(i, i ^ (2 * flip)) for i in range(shards)])

    def swap(value):
        return lax.ppermute(value, "shard", [(i, i ^ 1) for i in range(shards)])

    def onward(value):
        return lax.ppermute(value, "section", [(s, (s + 1) % sections) for s in range(sections)])

    section = lax.axis_index("section").astype(jnp.int32).reshape(1)
    info, packed = pl.pallas_call(
        pack_kernel,
        out_shape=[
            jax.ShapeDtypeStruct((MAIN, 128), bf16),
            jax.ShapeDtypeStruct((MAIN, model + model // SLABS), bf16),
        ],
        in_specs=[pl.BlockSpec(memory_space=pltpu.SMEM)] + [pl.BlockSpec(memory_space=pltpu.HBM)] * 3,
        out_specs=whole(2),
        scratch_shapes=[
            pltpu.VMEM(expert_ids.shape[:0:-1], jnp.int32),
            pltpu.VMEM(gate_probs.shape[:0:-1], f32),
            pltpu.VMEM((count, model), bf16),
            pltpu.SemaphoreType.DMA((3,)),
        ],
        compiler_params=params(),
        cost_estimate=cost(0, 4 * count * model),
        name="pack",
    )(section, in_hbm(expert_ids[0].T), in_hbm(gate_probs[0].T), in_hbm(rows[0]))

    mine = [packed] + [along(packed, m) for m in range(1, chips)]

    gate_w, up_w, down_w, done = pl.pallas_call(
        fetch_kernel,
        out_shape=[
            pltpu.VMEM((model, hidden_units), bf16),
            pltpu.VMEM((model, hidden_units), bf16),
            pltpu.VMEM((hidden_units, model), bf16),
            jax.ShapeDtypeStruct((8, 128), f32),
        ],
        in_specs=[pl.BlockSpec(memory_space=pl.ANY)] + [pl.BlockSpec(memory_space=pltpu.HBM)] * 3,
        out_specs=whole(4),
        scratch_shapes=[pltpu.SemaphoreType.DMA((3, 8))],
        compiler_params=pltpu.CompilerParams(vmem_limit_bytes=12*1024*1024),
        cost_estimate=cost(0, 3 * 2 * 2 * model * hidden_units),
        name="fetch",
    )(packed, in_hbm(w_gate[0]), in_hbm(w_up[0]), in_hbm(w_down[0]))
    rows_in = onward(rows[0])

    def stack(*blocks):
        return pl.pallas_call(
            lambda *refs: stack_kernel(len(blocks), *refs),
            out_shape=jax.ShapeDtypeStruct((len(blocks) * MAIN, model + model // SLABS), bf16),
            in_specs=whole(len(blocks)) + [pl.BlockSpec(memory_space=pl.ANY)],
            out_specs=pl.BlockSpec(memory_space=pltpu.VMEM),
            compiler_params=params(),
            name="stack",
        )(*blocks, done)

    held = [stack(*mine[: chips // 2]), stack(*mine[chips // 2 :])]
    hidden = pl.pallas_call(
        lambda *refs: hidden_kernel(shards, *refs),
        out_shape=jax.ShapeDtypeStruct((total_rows, hidden_units), bf16),
        in_specs=whole(6),
        out_specs=pl.BlockSpec(memory_space=pltpu.VMEM),
        scratch_shapes=[pltpu.VMEM((total_rows, model), bf16)],
        compiler_params=params(),
        cost_estimate=cost(4 * total_rows * model * hidden_units, 4 * model * hidden_units),
        name="hidden",
    )(gate_w, up_w, *held, *[swap(part) for part in held])

    halves = []
    for c, wide in enumerate(wides):
        own, other = pl.pallas_call(
            lambda *refs, c=c: down_kernel(shards, c, *refs),
            out_shape=[
                jax.ShapeDtypeStruct((chips * MAIN, wide), f32),
                jax.ShapeDtypeStruct((chips * MAIN, wide), bf16),
            ],
            in_specs=whole(2),
            out_specs=whole(2),
            compiler_params=params(),
            name="down",
        )(hidden, down_w)
        halves.append((own, swap(other)))
    arrived = []
    for c, (wide, (own, other)) in enumerate(zip(wides, halves)):
        last = c == len(CHUNKS) - 1
        kept, *leaving = pl.pallas_call(
            add_kernel,
            out_shape=[jax.ShapeDtypeStruct((MAIN, wide + 128 * last), bf16 if last else f32)]
            + [jax.ShapeDtypeStruct((MAIN, wide), bf16)] * (chips - 1),
            in_specs=whole(3),
            out_specs=whole(chips),
            compiler_params=params(),
            name="add_cores",
        )(own, other, info)
        if last:
            arrived += [across(block, m) for m, block in enumerate((kept, *leaving))]
            break
        coming = [along(leaving[m - 1], m) for m in (chips - 1, *range(1, chips - 1))]
        extra = []
        summed = pl.pallas_call(
            lambda *refs: sum_kernel(chips, *refs),
            out_shape=jax.ShapeDtypeStruct((MAIN, wide + 128 * len(extra)), bf16),
            in_specs=whole(chips + len(extra)),
            out_specs=pl.BlockSpec(memory_space=pltpu.VMEM),
            compiler_params=params(),
            name="sum_chips",
        )(kept, *coming, *extra)
        arrived.append(onward(summed))
    out = pl.pallas_call(
        combine_kernel,
        out_shape=jax.ShapeDtypeStruct((count, model), bf16),
        in_specs=whole(len(CHUNKS) + chips),
        out_specs=pl.BlockSpec(memory_space=pltpu.VMEM),
        compiler_params=params(),
        name="combine",
    )(rows_in, *arrived)
    return out[None]


def solution(mesh):
    in_specs = (
        P("section", "shard", None),
        P("section", "shard", None),
        P("section", "shard", None),
        P("section", None, "shard"),
        P("section", None, "shard"),
        P("section", "shard", None),
    )
    return jax.shard_map(
        on_device, mesh=mesh, in_specs=in_specs, out_specs=P("section", "shard", None), check_vma=False
    )
```
